768 devices in a mesh: dp: 64 (over z_hi, y, x), node: 12 (over z_lo, core).
Axes of the slice: x: 4, y: 8, z: 12 (z_hi: 2, z_lo: 6; z = z_hi * 6 + z_lo), core: 2. Of those that a mesh axis runs over, the one named last changes fastest.
Arguments:
- tokens: bfloat16 [98304, 4096], P(('dp', 'node')), may hold values from -6 to 6
- cotangent: bfloat16 [98304, 512], P(('dp', 'node')), may hold values from -6 to 6
- prim_values: bfloat16 [16896, 128], P(('dp', 'node')), may hold values from -0.09375 to 0.09375
- prim_scales: float32 [16896], P(('dp', 'node')), may hold values from 0.5 to 2
- sec_values: bfloat16 [4104, 512], P('node'), may hold values from -0.09375 to 0.09375
- sec_scales: float32 [4104], P('node'), may hold values from 0.5 to 2
Outputs:
- keys: bfloat16 [98304, 512], P(('dp', 'node'))
- input_grad: bfloat16 [98304, 4096], P(('dp', 'node'))
- weight_grad: float32 [16896, 128], P(('dp', 'node'))
The draws below stay inside these ranges and needn't reach their ends.
All inputs are finite; a program needn't handle non-finite values.
Results may differ from the reference program's by a relative error of at most 0.019.
Values may be sent and summed in bfloat16 or wider, within the bound.
A program may use at most 64 MiB of HBM per device.

```python
import math
import jax
import jax.numpy as jnp
from jax import lax

D = 4096
F = 512
TOK_DEV = 128
BLOCKS = 16384
PRIM_DEV = 22
SEC_ROWS = 342
TOKENS = 98304
N_DP = 64
N_NODE = 12
DEVICES = 768


def level_of(own_key, extent, shards, least, high):
    factor_of = 1.0
    for axis_at, parts in shards:
        steps = jax.random.uniform(jax.random.fold_in(jax.random.fold_in(own_key, 6), axis_at), (parts,), jnp.float32, least / len(shards), high / len(shards))
        factor_of = factor_of * jnp.repeat(jnp.exp(steps), extent[axis_at] // parts).reshape((-1,) + (1,) * (len(extent) - 1 - axis_at))
    return factor_of


def scatter_about(stream_key, dims, scale, bound, split=(), held_as=jnp.bfloat16):
    drawn = scale * jax.random.normal(stream_key, dims, jnp.float32)
    if split:
        drawn = drawn * level_of(stream_key, dims, split, -0.22, 0.18)
    return jnp.clip(drawn, -bound, bound).astype(held_as)


def setup_inputs(seed: int = 0) -> dict:
    streams_of = jax.random.split(jax.random.key(seed), 7)
    tokens = scatter_about(streams_of[0], (TOKENS, D), 1.0, 6.0, ((0, 768),))
    cotangent = scatter_about(streams_of[1], (TOKENS, F), 1.0, 6.0, ((0, 768),))
    prim_values = scatter_about(streams_of[2], (PRIM_DEV * N_DP * N_NODE, 128), D ** -0.5, 0.09375, ((0, 768),))
    prim_scales = jnp.clip(jnp.exp(math.log(2.0) - 1.3862944 * jax.random.uniform(streams_of[3], (PRIM_DEV * N_DP * N_NODE,), jnp.float32) ** level_of(streams_of[3], (PRIM_DEV * N_DP * N_NODE,), ((0, 768),), -0.2, 0.2)), 0.5, 2.0)
    sec_values = scatter_about(streams_of[4], (SEC_ROWS * N_NODE, F), D ** -0.5, 0.09375, ((0, 12),))
    sec_scales = jnp.clip(jnp.exp(math.log(2.0) - 1.3862944 * jax.random.uniform(streams_of[5], (SEC_ROWS * N_NODE,), jnp.float32) ** level_of(streams_of[5], (SEC_ROWS * N_NODE,), ((0, 12),), -0.2, 0.2)), 0.5, 2.0)
    return dict(tokens=tokens, cotangent=cotangent, prim_values=prim_values, prim_scales=prim_scales, sec_values=sec_values, sec_scales=sec_scales)


def dequantize(values, scales):
    rows = values[:BLOCKS].astype(jnp.float32) * scales[:BLOCKS][:, None]
    return rows.astype(jnp.bfloat16).reshape(D, F)

def dequantize_rows(values, scales):
    rows = values[:D].astype(jnp.float32) * scales[:D][:, None]
    return rows.astype(jnp.bfloat16)

def reference(tokens, cotangent, prim_values, prim_scales, sec_values, sec_scales):
    w_fwd = dequantize(prim_values, prim_scales)
    keys = jnp.dot(tokens, w_fwd, preferred_element_type=jnp.float32).astype(jnp.bfloat16)
    w_bwd = dequantize_rows(sec_values, sec_scales)
    input_grad = jnp.dot(cotangent, w_bwd.T, preferred_element_type=jnp.float32).astype(jnp.bfloat16)
    groups = TOKENS // TOK_DEV
    tok_groups = tokens.reshape(groups, TOK_DEV, D)
    cot_groups = cotangent.reshape(groups, TOK_DEV, F)

    def accumulate(total, pair):
        term = jnp.dot(pair[0].T, pair[1], preferred_element_type=jnp.float32)
        term = term.astype(jnp.bfloat16).astype(jnp.float32)
        return (total + term, None)
    total, unused = lax.scan(accumulate, jnp.zeros((D, F), jnp.float32), (tok_groups, cot_groups))
    scaled = total * (1.0 / jnp.sqrt(jnp.float32(TOKENS)))
    flat = scaled.reshape(BLOCKS, 128)
    padding = jnp.zeros((PRIM_DEV * DEVICES - BLOCKS, 128), jnp.float32)
    weight_grad = jnp.concatenate([flat, padding], axis=0)
    return (keys, input_grad, weight_grad)
```

```python
import jax
import jax.numpy as jnp
from jax import lax
from jax.experimental import pallas as pl
from jax.experimental.pallas import tpu as pltpu
from jax.sharding import PartitionSpec as P

MESH = pl.DeviceIdType.MESH
BF = jnp.bfloat16
F32 = jnp.float32

NX, NY, NZ = 4, 8, 12
ROWS = 144
HALF = 256
SLAB = NX * ROWS
SEC = 368
SEC_A = 192
DEPTHS = (2, 2, 1)


def iota(shape, axis):
    return lax.broadcasted_iota(jnp.int32, shape, axis)


def one_hot(hit):
    return jnp.where(hit, 1.0, 0.0).astype(BF)


def line_of(k, half):
    z, core, h, i = k // 32, (k // 16) % 2, (k // 8) % 2, k % 8
    return jnp.where((i < 6) & (h == half), 11 * z + 5 * core + i, -1)


def dot(a, b):
    return jnp.dot(a, b, preferred_element_type=F32)


def kernel(
    tok, cot, wp, ws, keys, igrad, wgrad,
    te, wf, wst, gs, gr, gx, xr1, xr2, gy, yr, pz, pr, qz, qr, acc, wn,
    pz_s, pz_r, px_s, px_r, py_s, py_r, pc_s, pc_r,
    sz_s, sz_r, sc_s, sc_r,
    gc_s, gc_r, gx_s, gx_r, gy_s, gy_r, gz_s, gz_r,
):
    dp, nd = lax.axis_index("dp"), lax.axis_index("node")
    x, y, z, c = dp % 4, (dp // 4) % 8, (dp // 32) * 6 + nd // 2, nd % 2
    o = 1 - c
    zl = nd // 2

    def dev(dx=0, dy=0, dz=0, core=None):
        xx, yy, zz = (x + dx) % NX, (y + dy) % NY, (z + dz) % NZ
        return ((zz // 6) * 32 + yy * 4 + xx, (zz % 6) * 2 + (c if core is None else core))

    sent = []

    def copy(src, dst, ssem, rsem, target):
        return pltpu.make_async_remote_copy(
            src_ref=src, dst_ref=dst, send_sem=ssem, recv_sem=rsem,
            device_id=target, device_id_type=MESH,
        )

    def send(src, dst, ssem, rsem, target):
        one = copy(src, dst, ssem, rsem, target)
        one.start()
        sent.append(one)

    def landed(dst, ssem, rsem):
        copy(dst, dst, ssem, rsem, dev(core=o)).wait_recv()

    z_partners = [(d, rel) for d in range(NZ) for rel in (0, 1) if (d, rel) != (0, 0)]
    z_partners.sort(key=lambda t: -min(t[0], NZ - t[0]))

    barrier = pltpu.get_barrier_semaphore()
    count = 0
    for d, rel in z_partners:
        pl.semaphore_signal(barrier, inc=1, device_id=dev(dz=d, core=o if rel else c), device_id_type=MESH)
        count += 1
    for d in range(1, NX):
        pl.semaphore_signal(barrier, inc=1, device_id=dev(dx=d), device_id_type=MESH)
        count += 1
    for d in range(1, NY):
        pl.semaphore_signal(barrier, inc=1, device_id=dev(dy=d), device_id_type=MESH)
        count += 1

    k = iota((32, 32), 0)
    want = 4 * (k % 8) + 2 * (k // 16) + (k // 8) % 2 - 2 * c
    keep = (k % 8 < 6) & (want >= 0) & (want < 22)
    pick = one_hot(keep & (iota((32, 32), 1) == want))
    pz[...] = dot(pick, wp[...]).astype(BF).reshape(2, 16, 128)
    wst[nd] = ws[...]

    pl.semaphore_wait(barrier, count)

    for d, rel in z_partners:
        to = o if rel else c
        at = d * 2 + rel
        send(pz.at[to], pr.at[z, c], pz_s.at[at], pz_r.at[at], dev(dz=d, core=to))
    pr[z, c] = pz[c]

    def sec_part(n, piece):
        return wst.at[n, pl.ds(0, SEC_A)] if piece == 0 else wst.at[n, pl.ds(SEC_A, SEC - SEC_A)]

    def sec_node(side, hop):
        return ((zl - hop + 6) % 6 if side == 0 else (zl + hop) % 6) * 2

    def sec_index(side, hop, piece):
        return side * 6 + (hop - 1) * 2 + piece

    def sec_send(side, hop, piece):
        part = sec_part(sec_node(side, hop - 1) + c, piece)
        at = sec_index(side, hop, piece)
        send(part, part, sz_s.at[at], sz_r.at[at], dev(dz=1 if side == 0 else -1 + NZ))

    def sec_cross(side, hop, piece):
        part = sec_part(sec_node(side, hop) + c, piece)
        at = sec_index(side, hop, piece) if hop else 12 + piece
        send(part, part, sc_s.at[at], sc_r.at[at], dev(core=o))

    def sec_arrive(hop, order):
        for side in (0, 1):
            piece = side ^ order
            at = sec_index(side, hop, piece)
            landed(sec_part(sec_node(side, hop) + c, piece), sz_s.at[at], sz_r.at[at])
            if hop == 1 or (hop == 2 and order == 0):
                sec_send(side, hop + 1, piece)
            sec_cross(side, hop, piece)

    for order in (0, 1):
        for side in (0, 1):
            sec_send(side, 1, side ^ order)
    for piece in (0, 1):
        sec_cross(0, 0, piece)

    d = iota((1, SLAB), 1)
    xx = (d >= ROWS).astype(jnp.int32) + (d >= 2 * ROWS).astype(jnp.int32) + (d >= 3 * ROWS).astype(jnp.int32)
    j = d - ROWS * xx
    low = jnp.where(j < 66, 66 * xx + j, -100000)
    high = jnp.where((j >= 66) & (j < 132), 66 * xx + j - 66, -100000)
    for yy in range(NY):
        total = None
        for start, base in ((264 * yy, low), (2112 + 264 * yy, high)):
            a = start // 128 * 128
            wide = min(384, 4096 - a)
            sel = one_hot(iota((wide, SLAB), 0) == base + (start - a))
            part = dot(tok[:, a:a + wide], sel)
            total = part if total is None else total + part
        te[yy] = total.astype(BF)

    for d, rel in z_partners:
        at = d * 2 + rel
        landed(pr.at[(z - d + NZ) % NZ, o if rel else c], pz_s.at[at], pz_r.at[at])
    packets = pr[...].reshape(NZ * 32, 128)
    k = iota((ROWS, NZ * 32), 1)
    r = iota((ROWS, NZ * 32), 0)
    for h in (0, 1):
        wf[c, y, x, :, 128 * h:128 * h + 128] = dot(one_hot(line_of(k, h) == r), packets).astype(BF)
    for d in range(1, NX):
        own = wf.at[c, y, x]
        send(own, own, px_s.at[d], px_r.at[d], dev(dx=d))

    def grad(yy, core):
        part = cot[:, pl.ds(pl.multiple_of(core * HALF, HALF), HALF)]
        out = lax.dot_general(te[yy], part, (((0,), (0,)), ((), ())), preferred_element_type=F32)
        return out.reshape(NX, ROWS, HALF)

    def pair(ref, p):
        return ref.at[:, pl.ds(2 * p, 2)]

    ORDER = (0, 2, 1, 3)
    for p in ORDER:
        for yy in (2 * p, 2 * p + 1):
            gs[:, yy] = grad(yy, o).astype(BF)
        send(pair(gs, p), pair(gr, p), gc_s.at[p], gc_r.at[p], dev(core=o))

    def pri_part(core, side, hop, piece):
        yy = (y - hop + NY) % NY if side == 0 else (y + hop) % NY
        return wf.at[core, yy, pl.ds(2 * piece, 2)]

    def pri_send(side, hop, piece):
        part = pri_part(c, side, hop - 1, piece)
        at = side * 8 + (hop - 1) * 2 + piece
        send(part, part, py_s.at[at], py_r.at[at], dev(dy=1 if side == 0 else NY - 1))

    def pri_cross_at(side, hop, piece):
        return side * 8 + (hop - 1) * 2 + piece if hop else 16 + piece

    def pri_cross(side, hop, piece):
        part = pri_part(c, side, hop, piece)
        at = pri_cross_at(side, hop, piece)
        send(part, part, pc_s.at[at], pc_r.at[at], dev(core=o))

    def pri_arrive(hop, order):
        for side in (0, 1):
            piece = side ^ order
            at = side * 8 + (hop - 1) * 2 + piece
            landed(pri_part(c, side, hop, piece), py_s.at[at], py_r.at[at])
            if hop < 3 or (hop == 3 and order == 0):
                pri_send(side, hop + 1, piece)
            pri_cross(side, hop, piece)

    for d in range(1, NX):
        landed(wf.at[c, y, (x - d + NX) % NX], px_s.at[d], px_r.at[d])
    for order in (0, 1):
        for side in (0, 1):
            pri_send(side, 1, side ^ order)
    for piece in (0, 1):
        pri_cross(0, 0, piece)

    def x_send(side, stage, p):
        far = (x + 2) % NX
        near = (x + 1) % NX if side == 0 else (x + NX - 1) % NX
        src = gx.at[far if stage == 0 else near, pl.ds(2 * p, 2)]
        dst = xr1.at[side, pl.ds(2 * (p % 2), 2)] if stage == 0 else xr2.at[side, pl.ds(2 * p, 2)]
        at = side * 6 + (p % 2 if stage == 0 else 2 + p)
        send(src, dst, gx_s.at[at], gx_r.at[at], dev(dx=1 if side == 0 else NX - 1))

    def x_turn(p):
        side = p // 2
        at = side * 6 + p % 2
        landed(xr1.at[side, pl.ds(2 * (p % 2), 2)], gx_s.at[at], gx_r.at[at])
        near = (x + 1) % NX if side == 0 else (x + NX - 1) % NX
        for yy in (0, 1):
            gx[near, 2 * p + yy] = (
                gx[near, 2 * p + yy].astype(F32) + xr1[side, 2 * (p % 2) + yy].astype(F32)
            ).astype(BF)
        x_send(side, 1, p)

    def own_half(p):
        mine = [grad(yy, c) for yy in (2 * p, 2 * p + 1)]
        landed(pair(gr, p), gc_s.at[p], gc_r.at[p])
        for i in (0, 1):
            yy = 2 * p + i
            gx[:, yy] = (mine[i] + gr[:, yy].astype(F32)).astype(BF)
        side = p // 2
        x_send(side, 0, p)
        x_send(1 - side, 1, p)

    own_half(0)
    sec_arrive(1, 0)
    own_half(2)
    own_half(1)
    sec_arrive(1, 1)
    own_half(3)
    pri_arrive(1, 0)
    x_turn(0)
    x_turn(2)
    sec_arrive(2, 0)
    pri_arrive(1, 1)
    x_turn(1)
    x_turn(3)
    sec_arrive(2, 1)
    pri_arrive(2, 0)
    pri_arrive(2, 1)
    sec_arrive(3, 0)

    def y_sum(p):
        for side in (0, 1):
            at = side * 6 + 2 + p
            landed(xr2.at[side, pl.ds(2 * p, 2)], gx_s.at[at], gx_r.at[at])
        for yy in (2 * p, 2 * p + 1):
            gy[yy] = (gx[x, yy].astype(F32) + xr2[0, yy].astype(F32) + xr2[1, yy].astype(F32)).astype(BF)

    for p in ORDER:
        y_sum(p)
    for d in (4, 3, 5, 2, 6, 1, 7):
        send(gy.at[(y + d) % NY], yr.at[y], gy_s.at[d], gy_r.at[d], dev(dy=d))
    yr[y] = gy[y]
    pri_arrive(3, 0)
    pri_arrive(3, 1)
    pri_arrive(4, 0)

    for d in range(1, NY):
        landed(yr.at[(y - d + NY) % NY], gy_s.at[d], gy_r.at[d])
    line = yr[0].astype(F32)
    for yy in range(1, NY):
        line = line + yr[yy].astype(F32)
    line = line.astype(BF)
    k = iota((NZ * 32, ROWS), 0)
    r = iota((NZ * 32, ROWS), 1)
    packets = dot(one_hot(line_of(k, 0) == r), line[:, :128]) + dot(one_hot(line_of(k, 1) == r), line[:, 128:])
    qz[...] = packets.astype(BF).reshape(NZ, 2, 16, 128)
    for d, rel in z_partners:
        to = o if rel else c
        at = d * 2 + rel
        send(qz.at[(z + d) % NZ, to], qr.at[z, c], gz_s.at[at], gz_r.at[at], dev(dz=d, core=to))
    qr[z, c] = qz[z, c]

    for piece in (0, 1):
        landed(sec_part(zl * 2 + o, piece), sc_s.at[12 + piece], sc_r.at[12 + piece])
        for hop in (1, 2):
            for side in (0, 1):
                at = sec_index(side, hop, piece)
                landed(sec_part(sec_node(side, hop) + o, piece), sc_s.at[at], sc_r.at[at])
        at = sec_index(piece, 3, piece)
        landed(sec_part(sec_node(piece, 3) + o, piece), sc_s.at[at], sc_r.at[at])

    for t in range(256):
        parts = []
        for n in range(12):
            first = 342 * n // 16
            if 342 * n < 16 * t + 16 and 342 * n + 342 > 16 * t:
                parts.append(wst[n, 16 * (t - first):16 * (t - first) + 16])
        tile = parts[0] if len(parts) == 1 else (parts[0].astype(F32) + parts[1].astype(F32)).astype(BF)
        wn[16 * t:16 * t + 16] = tile
    for i in range(8):
        igrad[:, 512 * i:512 * i + 512] = lax.dot_general(
            cot[...], wn[512 * i:512 * i + 512], (((1,), (1,)), ((), ())), preferred_element_type=F32
        ).astype(BF)

    for piece in (0, 1):
        at = 16 + piece
        landed(pri_part(o, 0, 0, piece), pc_s.at[at], pc_r.at[at])
        for side in (0, 1):
            for hop in (1, 2, 3):
                at = pri_cross_at(side, hop, piece)
                landed(pri_part(o, side, hop, piece), pc_s.at[at], pc_r.at[at])
        at = pri_cross_at(piece, 4, piece)
        landed(pri_part(o, piece, 4, piece), pc_s.at[at], pc_r.at[at])
    for core in (0, 1):
        total = None
        for yy in range(NY):
            part = dot(te[yy], wf[core, yy].reshape(SLAB, HALF))
            total = part if total is None else total + part
        keys[:, HALF * core:HALF * core + HALF] = total.astype(BF)

    for d, rel in z_partners:
        at = d * 2 + rel
        landed(qr.at[(z - d + NZ) % NZ, o if rel else c], gz_s.at[at], gz_r.at[at])
    total = qr[0].astype(F32)
    for zz in range(1, NZ):
        total = total + qr[zz].astype(F32)
    total = total.reshape(32, 128)
    k = iota((24, 32), 1)
    want = 4 * (k % 8) + 2 * (k // 16) + (k // 8) % 2 - 2 * c
    pick = jnp.where((k % 8 < 6) & (iota((24, 32), 0) == want), 1.0, 0.0)
    acc[...] = lax.dot_general(
        pick, total, (((1,), (0,)), ((), ())), preferred_element_type=F32, precision=lax.Precision.HIGHEST
    )
    scale = 1.0 / jnp.sqrt(F32(128 * NX * NY * NZ * 2))
    wgrad[...] = acc[:22] * scale

    for one in sent:
        one.wait_send()


def local(tokens, cotangent, prim_values, prim_scales, sec_values, sec_scales):
    wp = (prim_values.astype(F32) * prim_scales[:, None]).astype(BF)
    wp = jnp.pad(wp, ((0, 10), (0, 0)))
    ws = (sec_values.astype(F32) * sec_scales[:, None]).astype(BF)
    shift = (6 * lax.axis_index("node")) % 16
    ws = lax.dynamic_update_slice(jnp.zeros((SEC, 512), BF), ws, (shift, 0))
    dma = pltpu.SemaphoreType.DMA
    vmem = pl.BlockSpec(memory_space=pltpu.VMEM)
    groups = [24, 4, 16, 18, 12, 14, 4, 12, 8, 24]
    return pl.pallas_call(
        kernel,
        name="sharded_projection",
        out_shape=(
            jax.ShapeDtypeStruct((128, 512), BF),
            jax.ShapeDtypeStruct((128, 4096), BF),
            jax.ShapeDtypeStruct((22, 128), F32),
        ),
        in_specs=[vmem] * 4,
        out_specs=(vmem, vmem, vmem),
        scratch_shapes=[
            pltpu.VMEM((NY, 128, SLAB), BF),
            pltpu.VMEM((2, NY, NX, ROWS, HALF), BF),
            pltpu.VMEM((12, SEC, 512), BF),
            pltpu.VMEM((NX, NY, ROWS, HALF), BF),
            pltpu.VMEM((NX, NY, ROWS, HALF), BF),
            pltpu.VMEM((NX, NY, ROWS, HALF), BF),
            pltpu.VMEM((2, 4, ROWS, HALF), BF),
            pltpu.VMEM((2, NY, ROWS, HALF), BF),
            pltpu.VMEM((NY, ROWS, HALF), BF),
            pltpu.VMEM((NY, ROWS, HALF), BF),
            pltpu.VMEM((2, 16, 128), BF),
            pltpu.VMEM((NZ, 2, 16, 128), BF),
            pltpu.VMEM((NZ, 2, 16, 128), BF),
            pltpu.VMEM((NZ, 2, 16, 128), BF),
            pltpu.VMEM((24, 128), F32),
            pltpu.VMEM((4096, 512), BF),
        ]
        + [dma((n,)) for n in groups for _ in (0, 1)],
        compiler_params=pltpu.CompilerParams(
            collective_id=0, has_side_effects=True, vmem_limit_bytes=52 * 2**20
        ),
    )(tokens, cotangent, wp, ws)


def solution(mesh):
    return jax.shard_map(
        local,
        mesh=mesh,
        in_specs=(
            P(("dp", "node"), None),
            P(("dp", "node"), None),
            P(("dp", "node"), None),
            P(("dp", "node")),
            P("node", None),
            P("node"),
        ),
        out_specs=(P(("dp", "node"), None), P(("dp", "node"), None), P(("dp", "node"), None)),
        check_vma=False,
    )
```

```python
import jax
import jax.numpy as jnp
from jax import lax
from jax.experimental import pallas as pl
from jax.experimental.pallas import tpu as pltpu
from jax.sharding import PartitionSpec as P

MESH = pl.DeviceIdType.MESH
BF = jnp.bfloat16
F32 = jnp.float32

NX, NY, NZ = 4, 8, 12
ROWS = 144
HALF = 256
SLAB = NX * ROWS
LANES = 128
SEC = 368
SEC_A = 192
RING = (4, 3, 5, 2, 6, 1, 7, 0)
PLACE = {r: k for k, r in enumerate(RING)}


def iota(shape, axis):
    return lax.broadcasted_iota(jnp.int32, shape, axis)


def one_hot(hit):
    return jnp.where(hit, 1.0, 0.0).astype(BF)


def line_of(k, half):
    z, core, h, i = k // 32, (k // 16) % 2, (k // 8) % 2, k % 8
    return jnp.where((i < 6) & (h == half), 11 * z + 5 * core + i, -1)


def dot(a, b):
    return jnp.dot(a, b, preferred_element_type=F32)


def kernel(
    tok, cot, pv, ps, sv, sc, keys, igrad, wgrad,
    te, wf0, wf1, wst, gs, gr, gx0, gx1, xr1, xr2, gy, yr, g1r, hx, xr3, pz, pr, qz, qr, acc, wn,
    pz_s, pz_r, px_s, px_r, py_s, py_r, pc_s, pc_r, ru_s, ru_r, rx_s, rx_r, rc_s, rc_r,
    sz_s, sz_r, sc_s, sc_r,
    gc_s, gc_r, gx_s, gx_r, gy_s, gy_r, hy_s, hy_r, hx_s, hx_r, gz_s, gz_r,
):
    dp, nd = lax.axis_index("dp"), lax.axis_index("node")
    x, y, z, c = dp % 4, (dp // 4) % 8, (dp // 32) * 6 + nd // 2, nd % 2
    o = 1 - c
    zl = nd // 2

    def dev(dx=0, dy=0, dz=0, core=None):
        xx, yy, zz = (x + dx) % NX, (y + dy) % NY, (z + dz) % NZ
        return ((zz // 6) * 32 + yy * 4 + xx, (zz % 6) * 2 + (c if core is None else core))

    sent = []

    def copy(src, dst, ssem, rsem, target):
        return pltpu.make_async_remote_copy(
            src_ref=src, dst_ref=dst, send_sem=ssem, recv_sem=rsem,
            device_id=target, device_id_type=MESH,
        )

    def send(src, dst, ssem, rsem, target):
        one = copy(src, dst, ssem, rsem, target)
        one.start()
        sent.append(one)

    def landed(dst, ssem, rsem):
        copy(dst, dst, ssem, rsem, dev(core=o)).wait_recv()

    z_partners = [(d, rel) for d in range(NZ) for rel in (0, 1) if (d, rel) != (0, 0)]
    z_partners.sort(key=lambda t: -min(t[0], NZ - t[0]))

    barrier = pltpu.get_barrier_semaphore()
    count = 0
    for d, rel in z_partners:
        pl.semaphore_signal(barrier, inc=1, device_id=dev(dz=d, core=o if rel else c), device_id_type=MESH)
        count += 1
    for d in range(1, NY):
        pl.semaphore_signal(barrier, inc=1, device_id=dev(dy=d), device_id_type=MESH)
        count += 1
    for d in range(1, NX):
        pl.semaphore_signal(barrier, inc=1, device_id=dev(dx=d), device_id_type=MESH)
        count += 1

    k = iota((32, 22), 0)
    want = 4 * (k % 8) + 2 * (k // 16) + (k // 8) % 2 - 2 * c
    hit = (k % 8 < 6) & (iota((32, 22), 1) == want)
    factor = jnp.sum(jnp.where(hit, ps[...], 0.0), axis=1, keepdims=True)
    pz[...] = (dot(one_hot(hit), pv[...]) * factor).astype(BF).reshape(2, 16, 128)

    pl.semaphore_wait(barrier, count)

    for d, rel in z_partners:
        to = o if rel else c
        at = d * 2 + rel
        send(pz.at[to], pr.at[z, c], pz_s.at[at], pz_r.at[at], dev(dz=d, core=to))
    pr[z, c] = pz[c]

    hit = iota((SEC, 342), 1) == iota((SEC, 342), 0) - (6 * nd) % 16
    factor = jnp.sum(jnp.where(hit, sc[...], 0.0), axis=1, keepdims=True)
    wst[nd] = (dot(one_hot(hit), sv[...]) * factor).astype(BF)

    def sec_part(n, piece):
        return wst.at[n, pl.ds(0, SEC_A)] if piece == 0 else wst.at[n, pl.ds(SEC_A, SEC - SEC_A)]

    def sec_node(side, hop):
        return ((zl - hop + 6) % 6 if side == 0 else (zl + hop) % 6) * 2

    def sec_index(side, hop, piece):
        return side * 6 + (hop - 1) * 2 + piece

    def sec_send(side, hop, piece):
        part = sec_part(sec_node(side, hop - 1) + c, piece)
        at = sec_index(side, hop, piece)
        send(part, part, sz_s.at[at], sz_r.at[at], dev(dz=1 if side == 0 else NZ - 1))

    def sec_cross(side, hop, piece):
        part = sec_part(sec_node(side, hop) + c, piece)
        at = sec_index(side, hop, piece) if hop else 12 + piece
        send(part, part, sc_s.at[at], sc_r.at[at], dev(core=o))

    def sec_arrive(hop, order):
        for side in (0, 1):
            piece = side ^ order
            at = sec_index(side, hop, piece)
            landed(sec_part(sec_node(side, hop) + c, piece), sz_s.at[at], sz_r.at[at])
            if hop == 1 or (hop == 2 and order == 0):
                sec_send(side, hop + 1, piece)
            sec_cross(side, hop, piece)

    for order in (0, 1):
        for side in (0, 1):
            sec_send(side, 1, side ^ order)

    d = iota((1, SLAB), 1)
    xx = (d >= ROWS).astype(jnp.int32) + (d >= 2 * ROWS).astype(jnp.int32) + (d >= 3 * ROWS).astype(jnp.int32)
    j = d - ROWS * xx
    low = jnp.where(j < 66, 66 * xx + j, -100000)
    high = jnp.where((j >= 66) & (j < 132), 66 * xx + j - 66, -100000)
    for yy in range(NY):
        total = None
        for start, base in ((264 * yy, low), (2112 + 264 * yy, high)):
            a = start // 128 * 128
            wide = min(384, 4096 - a)
            sel = one_hot(iota((wide, SLAB), 0) == base + (start - a))
            part = dot(tok[:, a:a + wide], sel)
            total = part if total is None else total + part
        te[yy] = total.astype(BF)

    def grad(k, core):
        part = cot[:, pl.ds(pl.multiple_of(core * HALF, HALF), HALF)]
        rows = te[(y + RING[k]) % NY]
        out = lax.dot_general(rows, part, (((0,), (0,)), ((), ())), preferred_element_type=F32)
        return out.reshape(NX, ROWS, HALF)

    def give(k):
        gs[k] = grad(k, o).astype(BF)
        send(gs.at[k], gr.at[k], gc_s.at[k], gc_r.at[k], dev(core=o))

    for k in range(4):
        give(k)

    for d, rel in z_partners:
        at = d * 2 + rel
        landed(pr.at[(z - d + NZ) % NZ, o if rel else c], pz_s.at[at], pz_r.at[at])
    packets = pr[...].reshape(NZ * 32, 128)
    k = iota((ROWS, NZ * 32), 1)
    r = iota((ROWS, NZ * 32), 0)
    wf1[c, x, 0] = dot(one_hot(line_of(k, 1) == r), packets).astype(BF)
    wf0[c, 0, x] = dot(one_hot(line_of(k, 0) == r), packets).astype(BF)
    for d in (4, 3, 5, 2, 6, 1, 7):
        send(wf1.at[c, x, 0], wf1.at[c, x, NY - d], ru_s.at[d], ru_r.at[d], dev(dy=d))
    for d in (2, 1, 3):
        own = wf0.at[c, 0, x]
        send(own, own, px_s.at[d], px_r.at[d], dev(dx=d))

    for k in range(4, 8):
        give(k)
    sec_arrive(1, 0)

    def pri_part(core, side, hop, piece):
        return wf0.at[core, (NY - hop) % NY if side == 0 else hop, pl.ds(2 * piece, 2)]

    def pri_send(side, hop, piece):
        at = side * 8 + (hop - 1) * 2 + piece
        send(pri_part(c, side, hop - 1, piece), pri_part(c, side, hop, piece),
             py_s.at[at], py_r.at[at], dev(dy=1 if side == 0 else NY - 1))

    def pri_cross_at(side, hop, piece):
        return side * 8 + (hop - 1) * 2 + piece if hop else 16 + piece

    def pri_cross(side, hop, piece):
        part = pri_part(c, side, hop, piece)
        at = pri_cross_at(side, hop, piece)
        send(part, part, pc_s.at[at], pc_r.at[at], dev(core=o))

    def pri_arrive(hop, order):
        for side in (0, 1):
            piece = side ^ order
            at = side * 8 + (hop - 1) * 2 + piece
            landed(pri_part(c, side, hop, piece), py_s.at[at], py_r.at[at])
            if hop < 3 or (hop == 3 and order == 0):
                pri_send(side, hop + 1, piece)
            pri_cross(side, hop, piece)

    def pri_turn():
        for d in range(1, NX):
            landed(wf0.at[c, 0, (x - d + NX) % NX], px_s.at[d], px_r.at[d])
        for order in (0, 1):
            for side in (0, 1):
                pri_send(side, 1, side ^ order)
        for piece in (0, 1):
            pri_cross(0, 0, piece)

    def alt_part(core, side, hop, piece):
        xx = (x - hop + NX) % NX if side == 0 else (x + hop) % NX
        return wf1.at[core, xx, pl.ds(4 * piece, 4)]

    def alt_send(side, hop, piece):
        part = alt_part(c, side, hop - 1, piece)
        at = side * 4 + (hop - 1) * 2 + piece
        send(part, part, rx_s.at[at], rx_r.at[at], dev(dx=1 if side == 0 else NX - 1))

    def alt_cross_at(side, hop, piece):
        return side * 4 + (hop - 1) * 2 + piece if hop else 8 + piece

    def alt_cross(side, hop, piece):
        part = alt_part(c, side, hop, piece)
        at = alt_cross_at(side, hop, piece)
        send(part, part, rc_s.at[at], rc_r.at[at], dev(core=o))

    def alt_arrive(hop, order):
        for side in (0, 1):
            piece = side ^ order
            at = side * 4 + (hop - 1) * 2 + piece
            landed(alt_part(c, side, hop, piece), rx_s.at[at], rx_r.at[at])
            if hop == 1 and order == 0:
                alt_send(side, 2, piece)
            alt_cross(side, hop, piece)

    def alt_turn():
        for d in range(1, NY):
            landed(wf1.at[c, x, NY - d], ru_s.at[d], ru_r.at[d])
        for order in (0, 1):
            for side in (0, 1):
                alt_send(side, 1, side ^ order)
        for piece in (0, 1):
            alt_cross(0, 0, piece)

    def x_send(side, stage, p):
        far = (x + 2) % NX
        near = (x + 1) % NX if side == 0 else (x + NX - 1) % NX
        src = gx0.at[far if stage == 0 else near, pl.ds(2 * p, 2)]
        dst = xr1.at[side, pl.ds(2 * (p // 2), 2)] if stage == 0 else xr2.at[side, pl.ds(2 * p, 2)]
        at = side * 6 + (p // 2 if stage == 0 else 2 + p)
        send(src, dst, gx_s.at[at], gx_r.at[at], dev(dx=1 if side == 0 else NX - 1))

    def x_turn(p):
        side = p % 2
        at = side * 6 + p // 2
        landed(xr1.at[side, pl.ds(2 * (p // 2), 2)], gx_s.at[at], gx_r.at[at])
        near = (x + 1) % NX if side == 0 else (x + NX - 1) % NX
        for i in (0, 1):
            gx0[near, 2 * p + i] = (
                gx0[near, 2 * p + i].astype(F32) + xr1[side, 2 * (p // 2) + i].astype(F32)
            ).astype(BF)
        x_send(side, 1, p)

    def y_at(side, hop, piece):
        return side * 8 + (hop - 1) * 2 + piece

    def y_send(side, hop, piece):
        src = gx1.at[PLACE[5 - hop if side == 0 else 3 + hop], pl.ds(2 * piece, 2)]
        at = y_at(side, hop, piece)
        send(src, g1r.at[side, hop - 1, pl.ds(2 * piece, 2)], hy_s.at[at], hy_r.at[at],
             dev(dy=1 if side == 0 else NY - 1))

    def y_turn(side, hop, piece):
        at = y_at(side, hop, piece)
        part = pl.ds(2 * piece, 2)
        landed(g1r.at[side, hop - 1, part], hy_s.at[at], hy_r.at[at])
        k = PLACE[4 - hop if side == 0 else 4 + hop]
        gx1[k, part] = (gx1[k, part].astype(F32) + g1r[side, hop - 1, part].astype(F32)).astype(BF)
        y_send(side, hop + 1, piece)

    def own_half(p):
        for k in (2 * p, 2 * p + 1):
            mine = grad(k, c)
            landed(gr.at[k], gc_s.at[k], gc_r.at[k])
            mine = (mine + gr[k].astype(F32)).astype(BF)
            gx0[:, k] = mine[:, :, :LANES]
            gx1[k] = mine[:, :, LANES:]
            if RING[k] == 4:
                y_send(0, 1, 0)
                y_send(1, 1, 1)
            if RING[k] == 3:
                y_send(0, 2, 1)
            if RING[k] == 5:
                y_send(1, 2, 0)
        side = p % 2
        x_send(side, 0, p)
        x_send(1 - side, 1, p)

    own_half(0)
    own_half(1)
    pri_turn()
    own_half(2)
    own_half(3)
    sec_arrive(1, 1)
    for piece in (0, 1):
        sec_cross(0, 0, piece)
    x_turn(0)
    x_turn(1)
    y_turn(0, 1, 0)
    y_turn(1, 1, 1)
    alt_turn()
    pri_arrive(1, 0)
    sec_arrive(2, 0)
    y_turn(0, 2, 1)
    y_turn(1, 2, 0)
    x_turn(2)
    x_turn(3)
    pri_arrive(1, 1)
    y_turn(0, 2, 0)
    y_turn(1, 2, 1)
    pri_arrive(2, 0)
    y_turn(0, 3, 1)
    y_turn(1, 3, 0)
    sec_arrive(2, 1)
    pri_arrive(2, 1)
    alt_arrive(1, 0)
    y_turn(0, 3, 0)
    y_turn(1, 3, 1)

    for p in (0, 1, 2, 3):
        for side in (0, 1):
            at = side * 6 + 2 + p
            landed(xr2.at[side, pl.ds(2 * p, 2)], gx_s.at[at], gx_r.at[at])
        for k in (2 * p, 2 * p + 1):
            mine = (gx0[x, k].astype(F32) + xr2[0, k].astype(F32) + xr2[1, k].astype(F32)).astype(BF)
            if RING[k]:
                gy[k] = mine
                send(gy.at[k], yr.at[k], gy_s.at[k], gy_r.at[k], dev(dy=RING[k]))
            else:
                yr[k] = mine
    pri_arrive(3, 0)
    sec_arrive(3, 0)

    for piece in (1, 0):
        for side in (0, 1):
            at = y_at(side, 4, piece)
            landed(g1r.at[side, 3, pl.ds(2 * piece, 2)], hy_s.at[at], hy_r.at[at])
    hx[...] = (gx1[PLACE[0]].astype(F32) + g1r[0, 3].astype(F32) + g1r[1, 3].astype(F32)).astype(BF)
    for d in (2, 1, 3):
        send(hx.at[(x + d) % NX], xr3.at[d], hx_s.at[d], hx_r.at[d], dev(dx=d))
    xr3[0] = hx[x]
    alt_arrive(1, 1)
    pri_arrive(3, 1)
    alt_arrive(2, 0)
    pri_arrive(4, 0)

    for k in range(7):
        landed(yr.at[k], gy_s.at[k], gy_r.at[k])
    line0 = yr[0].astype(F32)
    for k in range(1, NY):
        line0 = line0 + yr[k].astype(F32)
    for d in range(1, NX):
        landed(xr3.at[d], hx_s.at[d], hx_r.at[d])
    line1 = xr3[0].astype(F32)
    for d in range(1, NX):
        line1 = line1 + xr3[d].astype(F32)
    k = iota((NZ * 32, ROWS), 0)
    r = iota((NZ * 32, ROWS), 1)
    packets = dot(one_hot(line_of(k, 0) == r), line0.astype(BF)) + dot(one_hot(line_of(k, 1) == r), line1.astype(BF))
    qz[...] = packets.astype(BF).reshape(NZ, 2, 16, 128)
    for d, rel in z_partners:
        to = o if rel else c
        at = d * 2 + rel
        send(qz.at[(z + d) % NZ, to], qr.at[z, c], gz_s.at[at], gz_r.at[at], dev(dz=d, core=to))
    qr[z, c] = qz[z, c]

    for piece in (0, 1):
        landed(sec_part(zl * 2 + o, piece), sc_s.at[12 + piece], sc_r.at[12 + piece])
        for hop in (1, 2):
            for side in (0, 1):
                at = sec_index(side, hop, piece)
                landed(sec_part(sec_node(side, hop) + o, piece), sc_s.at[at], sc_r.at[at])
        at = sec_index(piece, 3, piece)
        landed(sec_part(sec_node(piece, 3) + o, piece), sc_s.at[at], sc_r.at[at])

    for t in range(256):
        parts = []
        for n in range(12):
            first = 342 * n // 16
            if 342 * n < 16 * t + 16 and 342 * n + 342 > 16 * t:
                parts.append(wst[n, 16 * (t - first):16 * (t - first) + 16])
        tile = parts[0] if len(parts) == 1 else (parts[0].astype(F32) + parts[1].astype(F32)).astype(BF)
        wn[16 * t:16 * t + 16] = tile
    for i in range(8):
        igrad[:, 512 * i:512 * i + 512] = lax.dot_general(
            cot[...], wn[512 * i:512 * i + 512], (((1,), (1,)), ((), ())), preferred_element_type=F32
        ).astype(BF)

    for piece in (0, 1):
        at = 16 + piece
        landed(pri_part(o, 0, 0, piece), pc_s.at[at], pc_r.at[at])
        at = 8 + piece
        landed(alt_part(o, 0, 0, piece), rc_s.at[at], rc_r.at[at])
        for side in (0, 1):
            for hop in (1, 2, 3):
                at = pri_cross_at(side, hop, piece)
                landed(pri_part(o, side, hop, piece), pc_s.at[at], pc_r.at[at])
            at = alt_cross_at(side, 1, piece)
            landed(alt_part(o, side, 1, piece), rc_s.at[at], rc_r.at[at])
        at = pri_cross_at(piece, 4, piece)
        landed(pri_part(o, piece, 4, piece), pc_s.at[at], pc_r.at[at])
        at = alt_cross_at(piece, 2, piece)
        landed(alt_part(o, piece, 2, piece), rc_s.at[at], rc_r.at[at])
    for core in (0, 1):
        total = None
        for r in range(NY):
            w = jnp.concatenate([wf0[core, r].reshape(SLAB, LANES), wf1[core, :, r].reshape(SLAB, LANES)], axis=1)
            part = dot(te[(y + r) % NY], w)
            total = part if total is None else total + part
        keys[:, HALF * core:HALF * core + HALF] = total.astype(BF)

    for d, rel in z_partners:
        at = d * 2 + rel
        landed(qr.at[(z - d + NZ) % NZ, o if rel else c], gz_s.at[at], gz_r.at[at])
    total = qr[0].astype(F32)
    for zz in range(1, NZ):
        total = total + qr[zz].astype(F32)
    total = total.reshape(32, 128)
    k = iota((24, 32), 1)
    want = 4 * (k % 8) + 2 * (k // 16) + (k // 8) % 2 - 2 * c
    pick = jnp.where((k % 8 < 6) & (iota((24, 32), 0) == want), 1.0, 0.0)
    acc[...] = lax.dot_general(
        pick, total, (((1,), (0,)), ((), ())), preferred_element_type=F32, precision=lax.Precision.HIGHEST
    )
    scale = 1.0 / jnp.sqrt(F32(128 * NX * NY * NZ * 2))
    wgrad[...] = acc[:22] * scale

    for one in sent:
        one.wait_send()


def local(tokens, cotangent, prim_values, prim_scales, sec_values, sec_scales):
    dma = pltpu.SemaphoreType.DMA
    vmem = pl.BlockSpec(memory_space=pltpu.VMEM)
    groups = [24, 4, 16, 18, 8, 8, 10, 12, 14, 8, 12, 8, 16, 4, 24]
    return pl.pallas_call(
        kernel,
        name="sharded_projection",
        out_shape=(
            jax.ShapeDtypeStruct((128, 512), BF),
            jax.ShapeDtypeStruct((128, 4096), BF),
            jax.ShapeDtypeStruct((22, 128), F32),
        ),
        in_specs=[vmem] * 6,
        out_specs=(vmem, vmem, vmem),
        scratch_shapes=[
            pltpu.VMEM((NY, 128, SLAB), BF),
            pltpu.VMEM((2, NY, NX, ROWS, LANES), BF),
            pltpu.VMEM((2, NX, NY, ROWS, LANES), BF),
            pltpu.VMEM((12, SEC, 512), BF),
            pltpu.VMEM((NY, NX, ROWS, HALF), BF),
            pltpu.VMEM((NY, NX, ROWS, HALF), BF),
            pltpu.VMEM((NX, NY, ROWS, LANES), BF),
            pltpu.VMEM((NY, NX, ROWS, LANES), BF),
            pltpu.VMEM((2, 4, ROWS, LANES), BF),
            pltpu.VMEM((2, NY, ROWS, LANES), BF),
            pltpu.VMEM((NY, ROWS, LANES), BF),
            pltpu.VMEM((NY, ROWS, LANES), BF),
            pltpu.VMEM((2, 4, NX, ROWS, LANES), BF),
            pltpu.VMEM((NX, ROWS, LANES), BF),
            pltpu.VMEM((NX, ROWS, LANES), BF),
            pltpu.VMEM((2, 16, 128), BF),
            pltpu.VMEM((NZ, 2, 16, 128), BF),
            pltpu.VMEM((NZ, 2, 16, 128), BF),
            pltpu.VMEM((NZ, 2, 16, 128), BF),
            pltpu.VMEM((24, 128), F32),
            pltpu.VMEM((4096, 512), BF),
        ]
        + [dma((n,)) for n in groups for _ in (0, 1)],
        compiler_params=pltpu.CompilerParams(
            collective_id=0, has_side_effects=True, vmem_limit_bytes=52 * 2**20
        ),
    )(tokens, cotangent, prim_values, prim_scales.reshape(1, -1), sec_values, sec_scales.reshape(1, -1))


def solution(mesh):
    return jax.shard_map(
        local,
        mesh=mesh,
        in_specs=(
            P(("dp", "node"), None),
            P(("dp", "node"), None),
            P(("dp", "node"), None),
            P(("dp", "node")),
            P("node", None),
            P("node"),
        ),
        out_specs=(P(("dp", "node"), None), P(("dp", "node"), None), P(("dp", "node"), None)),
        check_vma=False,
    )
```

```python
import jax
import jax.numpy as jnp
from jax import lax
from jax.experimental import pallas as pl
from jax.experimental.pallas import tpu as pltpu
from jax.sharding import PartitionSpec as P

MESH = pl.DeviceIdType.MESH
BF = jnp.bfloat16
F32 = jnp.float32

NX, NY, NZ = 4, 8, 12
ROWS = 144
HALF = 256
SLAB = NX * ROWS
CUT = 64
LANES = 128
SEC = 368
SEC_A = 192
RING = (4, 3, 5, 2, 6, 1, 7, 0)
PLACE = {r: k for k, r in enumerate(RING)}


def iota(shape, axis):
    return lax.broadcasted_iota(jnp.int32, shape, axis)


def one_hot(hit):
    return jnp.where(hit, 1.0, 0.0).astype(BF)


def line_of(k, half):
    z, core, h, i = k // 32, (k // 16) % 2, (k // 8) % 2, k % 8
    return jnp.where((i < 6) & (h == half), 11 * z + 5 * core + i, -1)


def dot(a, b):
    return jnp.dot(a, b, preferred_element_type=F32)


def kernel(
    tok_in, cot_in, pv, ps, sv_in, sc, keys_out, igrad_out, wgrad,
    tok, cot, sv, keys, igrad, in_s,
    te, wf0, wf1, wst, gs, gr, gx0, gx1, xr1, xr2, gy, yr, g1r, hx, xr3, pz, pr, qz, qr, acc, wn,
    pz_s, pz_r, px_s, px_r, py_s, py_r, pc_s, pc_r, ru_s, ru_r, rx_s, rx_r, rc_s, rc_r,
    sz_s, sz_r, sc_s, sc_r,
    gc_s, gc_r, gx_s, gx_r, gy_s, gy_r, hy_s, hy_r, hx_s, hx_r, gz_s, gz_r,
):
    dp, nd = lax.axis_index("dp"), lax.axis_index("node")
    x, y, z, c = dp % 4, (dp // 4) % 8, (dp // 32) * 6 + nd // 2, nd % 2
    o = 1 - c
    zl = nd // 2

    def dev(dx=0, dy=0, dz=0, core=None):
        xx, yy, zz = (x + dx) % NX, (y + dy) % NY, (z + dz) % NZ
        return ((zz // 6) * 32 + yy * 4 + xx, (zz % 6) * 2 + (c if core is None else core))

    sent = []

    def copy(src, dst, ssem, rsem, target):
        return pltpu.make_async_remote_copy(
            src_ref=src, dst_ref=dst, send_sem=ssem, recv_sem=rsem,
            device_id=target, device_id_type=MESH,
        )

    def send(src, dst, ssem, rsem, target):
        one = copy(src, dst, ssem, rsem, target)
        one.start()
        sent.append(one)

    def landed(dst, ssem, rsem):
        copy(dst, dst, ssem, rsem, dev(core=o)).wait_recv()

    z_partners = [(d, rel) for d in range(NZ) for rel in (0, 1) if (d, rel) != (0, 0)]
    z_partners.sort(key=lambda t: -min(t[0], NZ - t[0]))

    loads = [
        pltpu.make_async_copy(src, dst, in_s.at[i])
        for i, (src, dst) in enumerate(((sv_in, sv), (tok_in, tok), (cot_in, cot)))
    ]
    for one in loads:
        one.start()

    barrier = pltpu.get_barrier_semaphore()
    count = 0
    for d, rel in z_partners:
        pl.semaphore_signal(barrier, inc=1, device_id=dev(dz=d, core=o if rel else c), device_id_type=MESH)
        count += 1
    for d in (1, 2, 6, 7):
        pl.semaphore_signal(barrier, inc=1, device_id=dev(dy=d), device_id_type=MESH)
        count += 1
    for d in range(1, NX):
        pl.semaphore_signal(barrier, inc=1, device_id=dev(dx=d), device_id_type=MESH)
        count += 1

    k = iota((32, 22), 0)
    want = 4 * (k % 8) + 2 * (k // 16) + (k // 8) % 2 - 2 * c
    hit = (k % 8 < 6) & (iota((32, 22), 1) == want)
    factor = jnp.sum(jnp.where(hit, ps[...], 0.0), axis=1, keepdims=True)
    pz[...] = (dot(one_hot(hit), pv[...]) * factor).astype(BF).reshape(2, 16, 128)

    loads[0].wait()
    hit = iota((SEC, 342), 1) == iota((SEC, 342), 0) - (6 * nd) % 16
    factor = jnp.sum(jnp.where(hit, sc[...][None, :], 0.0), axis=1, keepdims=True)
    wst[nd] = (dot(one_hot(hit), sv[...]) * factor).astype(BF)

    d = iota((1, SLAB), 1)
    xx = (d >= ROWS).astype(jnp.int32) + (d >= 2 * ROWS).astype(jnp.int32) + (d >= 3 * ROWS).astype(jnp.int32)
    j = d - ROWS * xx
    low = jnp.where(j < 66, 66 * xx + j, -100000)
    high = jnp.where((j >= 66) & (j < 132), 66 * xx + j - 66, -100000)
    loads[1].wait()
    loads[2].wait()
    for yy in range(NY):
        total = None
        for start, base in ((264 * yy, low), (2112 + 264 * yy, high)):
            a = start // 128 * 128
            wide = min(384, 4096 - a)
            sel = one_hot(iota((wide, SLAB), 0) == base + (start - a))
            part = dot(tok[:, a:a + wide], sel)
            total = part if total is None else total + part
        te[yy] = total.astype(BF)

    def grad(k, core):
        part = cot[:, pl.ds(pl.multiple_of(core * HALF, HALF), HALF)]
        rows = te[(y + RING[k]) % NY]
        out = lax.dot_general(rows, part, (((0,), (0,)), ((), ())), preferred_element_type=F32)
        return out.reshape(NX, ROWS, HALF)

    for k in range(8):
        gs[k] = grad(k, o).astype(BF)

    pl.semaphore_wait(barrier, count)

    for d, rel in z_partners:
        to = o if rel else c
        at = d * 2 + rel
        send(pz.at[to], pr.at[z, c], pz_s.at[at], pz_r.at[at], dev(dz=d, core=to))
    pr[z, c] = pz[c]

    for k in range(8):
        send(gs.at[k], gr.at[k], gc_s.at[k], gc_r.at[k], dev(core=o))

    def sec_part(n, piece):
        return wst.at[n, pl.ds(0, SEC_A)] if piece == 0 else wst.at[n, pl.ds(SEC_A, SEC - SEC_A)]

    def sec_node(side, hop):
        return ((zl - hop + 6) % 6 if side == 0 else (zl + hop) % 6) * 2

    def sec_index(side, hop, piece):
        return side * 6 + (hop - 1) * 2 + piece

    def sec_send(side, hop, piece):
        part = sec_part(sec_node(side, hop - 1) + c, piece)
        at = sec_index(side, hop, piece)
        send(part, part, sz_s.at[at], sz_r.at[at], dev(dz=1 if side == 0 else NZ - 1))

    def sec_cross(side, hop, piece):
        part = sec_part(sec_node(side, hop) + c, piece)
        at = sec_index(side, hop, piece) if hop else 12 + piece
        send(part, part, sc_s.at[at], sc_r.at[at], dev(core=o))

    def sec_arrive(hop, order):
        for side in (0, 1):
            piece = side ^ order
            at = sec_index(side, hop, piece)
            landed(sec_part(sec_node(side, hop) + c, piece), sz_s.at[at], sz_r.at[at])
            if hop == 1 or (hop == 2 and order == 0):
                sec_send(side, hop + 1, piece)
            sec_cross(side, hop, piece)

    for order in (0, 1):
        for side in (0, 1):
            sec_send(side, 1, side ^ order)

    def pri_part(core, side, hop, piece):
        return wf0.at[core, (NY - hop) % NY if side == 0 else hop, pl.ds(2 * piece, 2)]

    def pri_send(side, hop, piece):
        at = side * 8 + (hop - 1) * 2 + piece
        send(pri_part(c, side, hop - 1, piece), pri_part(c, side, hop, piece),
             py_s.at[at], py_r.at[at], dev(dy=1 if side == 0 else NY - 1))

    def pri_cross_at(side, hop, piece):
        return side * 8 + (hop - 1) * 2 + piece if hop else 16 + piece

    def pri_cross(side, hop, piece):
        part = pri_part(c, side, hop, piece)
        at = pri_cross_at(side, hop, piece)
        send(part, part, pc_s.at[at], pc_r.at[at], dev(core=o))

    def pri_arrive(hop, order):
        for side in (0, 1):
            piece = side ^ order
            at = side * 8 + (hop - 1) * 2 + piece
            landed(pri_part(c, side, hop, piece), py_s.at[at], py_r.at[at])
            if hop < 3 or (hop == 3 and order == 0):
                pri_send(side, hop + 1, piece)
            pri_cross(side, hop, piece)

    def pri_turn():
        for d in range(1, NX):
            landed(wf0.at[c, 0, (x - d + NX) % NX], px_s.at[d], px_r.at[d])
        for order in (0, 1):
            for side in (0, 1):
                pri_send(side, 1, side ^ order)
        for piece in (0, 1):
            pri_cross(0, 0, piece)

    def near_slot(side, far):
        r = NY - 1 - far if side == 0 else 1 + far
        if far < 3:
            return wf1.at[c, x, r]
        return wf1.at[c, x, r, pl.ds(0, CUT) if side == 0 else pl.ds(CUT, ROWS - CUT)]

    def near_send(side, far):
        slot = near_slot(side, far)
        if far < 2:
            src = wf1.at[c, x, 0]
        elif far == 2:
            src = near_slot(side, 1)
        else:
            src = wf1.at[c, x, 6 if side == 0 else 2, pl.ds(0, CUT) if side == 0 else pl.ds(CUT, ROWS - CUT)]
        at = side * 4 + far
        step = 2 if far in (1, 3) else 1
        send(src, slot, ru_s.at[at], ru_r.at[at], dev(dy=step if side == 0 else NY - step))

    def near_landed(side, far):
        at = side * 4 + far
        landed(near_slot(side, far), ru_s.at[at], ru_r.at[at])

    def alt_mid():
        for side in (0, 1):
            near_landed(side, 1)
            near_send(side, 3)
            near_send(side, 2)

    def alt_part(core, side, hop, piece):
        xx = (x - hop + NX) % NX if side == 0 else (x + hop) % NX
        return wf1.at[core, xx, pl.ds(4 * piece, 4)]

    def alt_send(side, hop, piece):
        part = alt_part(c, side, hop - 1, piece)
        at = side * 4 + (hop - 1) * 2 + piece
        send(part, part, rx_s.at[at], rx_r.at[at], dev(dx=1 if side == 0 else NX - 1))

    def alt_cross_at(side, hop, piece):
        return side * 4 + (hop - 1) * 2 + piece if hop else 8 + piece

    def alt_cross(side, hop, piece):
        part = alt_part(c, side, hop, piece)
        at = alt_cross_at(side, hop, piece)
        send(part, part, rc_s.at[at], rc_r.at[at], dev(core=o))

    def alt_arrive(hop, order):
        for side in (0, 1):
            piece = side ^ order
            at = side * 4 + (hop - 1) * 2 + piece
            landed(alt_part(c, side, hop, piece), rx_s.at[at], rx_r.at[at])
            if hop == 1 and order == 0:
                alt_send(side, 2, piece)
            alt_cross(side, hop, piece)

    def alt_turn():
        for far in (0, 2, 3):
            for side in (0, 1):
                near_landed(side, far)
        for order in (0, 1):
            for side in (0, 1):
                alt_send(side, 1, side ^ order)
        for piece in (0, 1):
            alt_cross(0, 0, piece)

    def x_send(side, stage, p):
        far = (x + 2) % NX
        near = (x + 1) % NX if side == 0 else (x + NX - 1) % NX
        src = gx0.at[far if stage == 0 else near, pl.ds(2 * p, 2)]
        dst = xr1.at[side, pl.ds(2 * (p // 2), 2)] if stage == 0 else xr2.at[side, pl.ds(2 * p, 2)]
        at = side * 6 + (p // 2 if stage == 0 else 2 + p)
        send(src, dst, gx_s.at[at], gx_r.at[at], dev(dx=1 if side == 0 else NX - 1))

    def x_turn(p):
        side = p % 2
        at = side * 6 + p // 2
        landed(xr1.at[side, pl.ds(2 * (p // 2), 2)], gx_s.at[at], gx_r.at[at])
        near = (x + 1) % NX if side == 0 else (x + NX - 1) % NX
        for i in (0, 1):
            gx0[near, 2 * p + i] = (
                gx0[near, 2 * p + i].astype(F32) + xr1[side, 2 * (p // 2) + i].astype(F32)
            ).astype(BF)
        x_send(side, 1, p)

    def y_at(side, hop, piece):
        return side * 8 + (hop - 1) * 2 + piece

    def y_send(side, hop, piece):
        src = gx1.at[PLACE[5 - hop if side == 0 else 3 + hop], pl.ds(2 * piece, 2)]
        at = y_at(side, hop, piece)
        send(src, g1r.at[side, hop - 1, pl.ds(2 * piece, 2)], hy_s.at[at], hy_r.at[at],
             dev(dy=1 if side == 0 else NY - 1))

    def y_turn(side, hop, piece):
        at = y_at(side, hop, piece)
        part = pl.ds(2 * piece, 2)
        landed(g1r.at[side, hop - 1, part], hy_s.at[at], hy_r.at[at])
        k = PLACE[4 - hop if side == 0 else 4 + hop]
        gx1[k, part] = (gx1[k, part].astype(F32) + g1r[side, hop - 1, part].astype(F32)).astype(BF)
        y_send(side, hop + 1, piece)

    def own_half(p):
        for k in (2 * p, 2 * p + 1):
            mine = grad(k, c)
            landed(gr.at[k], gc_s.at[k], gc_r.at[k])
            mine = (mine + gr[k].astype(F32)).astype(BF)
            gx0[:, k] = mine[:, :, :LANES]
            gx1[k] = mine[:, :, LANES:]
            if RING[k] == 4:
                y_send(0, 1, 0)
                y_send(1, 1, 1)
            if RING[k] == 3:
                y_send(0, 2, 1)
            if RING[k] == 5:
                y_send(1, 2, 0)
        side = p % 2
        x_send(side, 0, p)
        x_send(1 - side, 1, p)

    def pri_line():
        for d, rel in z_partners:
            at = d * 2 + rel
            landed(pr.at[(z - d + NZ) % NZ, o if rel else c], pz_s.at[at], pz_r.at[at])
        packets = pr[...].reshape(NZ * 32, 128)
        k = iota((ROWS, NZ * 32), 1)
        r = iota((ROWS, NZ * 32), 0)
        wf1[c, x, 0] = dot(one_hot(line_of(k, 1) == r), packets).astype(BF)
        wf0[c, 0, x] = dot(one_hot(line_of(k, 0) == r), packets).astype(BF)
        for far in (1, 0):
            for side in (0, 1):
                near_send(side, far)
        for d in (2, 1, 3):
            own = wf0.at[c, 0, x]
            send(own, own, px_s.at[d], px_r.at[d], dev(dx=d))

    own_half(0)
    own_half(1)
    pri_line()
    own_half(2)
    own_half(3)
    sec_arrive(1, 0)
    pri_turn()
    y_turn(0, 1, 0)
    y_turn(1, 1, 1)
    x_turn(0)
    x_turn(1)
    alt_mid()
    sec_arrive(1, 1)
    for piece in (0, 1):
        sec_cross(0, 0, piece)
    y_turn(0, 2, 1)
    y_turn(1, 2, 0)
    x_turn(2)
    x_turn(3)
    pri_arrive(1, 0)
    alt_turn()
    y_turn(0, 2, 0)
    y_turn(1, 2, 1)
    sec_arrive(2, 0)
    pri_arrive(1, 1)
    y_turn(0, 3, 1)
    y_turn(1, 3, 0)
    pri_arrive(2, 0)
    y_turn(0, 3, 0)
    y_turn(1, 3, 1)

    def fold_send(side, far, r):
        at = side * 4 + far
        k = PLACE[r]
        step = 2 if far in (1, 3) else 1
        part = pl.ds(0, ROWS) if far < 3 else (pl.ds(0, CUT) if side == 0 else pl.ds(CUT, ROWS - CUT))
        send(gy.at[k, part], yr.at[at, part], gy_s.at[at], gy_r.at[at], dev(dy=step if side == 0 else NY - step))

    def fold_landed(side, far):
        at = side * 4 + far
        part = pl.ds(0, ROWS) if far < 3 else (pl.ds(0, CUT) if side == 0 else pl.ds(CUT, ROWS - CUT))
        landed(yr.at[at, part], gy_s.at[at], gy_r.at[at])

    for p in (0, 1, 2, 3):
        for side in (0, 1):
            at = side * 6 + 2 + p
            landed(xr2.at[side, pl.ds(2 * p, 2)], gx_s.at[at], gx_r.at[at])
        for k in (2 * p, 2 * p + 1):
            gy[k] = (gx0[x, k].astype(F32) + xr2[0, k].astype(F32) + xr2[1, k].astype(F32)).astype(BF)
            r = RING[k]
            if r == 4:
                fold_send(0, 3, 4)
                fold_send(1, 3, 4)
            elif r in (3, 5):
                fold_send(0 if r == 3 else 1, 2, r)
            elif r in (1, 7):
                fold_send(0 if r == 1 else 1, 0, r)
    pri_arrive(2, 1)
    sec_arrive(2, 1)
    alt_arrive(1, 0)

    for piece in (1, 0):
        for side in (0, 1):
            at = y_at(side, 4, piece)
            landed(g1r.at[side, 3, pl.ds(2 * piece, 2)], hy_s.at[at], hy_r.at[at])
    hx[...] = (gx1[PLACE[0]].astype(F32) + g1r[0, 3].astype(F32) + g1r[1, 3].astype(F32)).astype(BF)
    for d in (2, 1, 3):
        send(hx.at[(x + d) % NX], xr3.at[d], hx_s.at[d], hx_r.at[d], dev(dx=d))
    xr3[0] = hx[x]

    for side in (0, 1):
        fold_landed(side, 2)
        fold_landed(side, 3)
        k = PLACE[2 if side == 0 else 6]
        gy[k] = (gy[k].astype(F32) + yr[side * 4 + 2].astype(F32)).astype(BF)
        part = pl.ds(0, CUT) if side == 0 else pl.ds(CUT, ROWS - CUT)
        gy[k, part] = (gy[k, part].astype(F32) + yr[side * 4 + 3, part].astype(F32)).astype(BF)
        fold_send(side, 1, 2 if side == 0 else 6)
    pri_arrive(3, 0)
    sec_arrive(3, 0)
    alt_arrive(1, 1)
    pri_arrive(3, 1)
    alt_arrive(2, 0)
    pri_arrive(4, 0)

    line0 = gy[PLACE[0]].astype(F32)
    for far in (0, 1):
        for side in (0, 1):
            fold_landed(side, far)
            line0 = line0 + yr[side * 4 + far].astype(F32)
    for d in range(1, NX):
        landed(xr3.at[d], hx_s.at[d], hx_r.at[d])
    line1 = xr3[0].astype(F32)
    for d in range(1, NX):
        line1 = line1 + xr3[d].astype(F32)
    k = iota((NZ * 32, ROWS), 0)
    r = iota((NZ * 32, ROWS), 1)
    packets = dot(one_hot(line_of(k, 0) == r), line0.astype(BF)) + dot(one_hot(line_of(k, 1) == r), line1.astype(BF))
    qz[...] = packets.astype(BF).reshape(NZ, 2, 16, 128)
    for d, rel in z_partners:
        to = o if rel else c
        at = d * 2 + rel
        send(qz.at[(z + d) % NZ, to], qr.at[z, c], gz_s.at[at], gz_r.at[at], dev(dz=d, core=to))
    qr[z, c] = qz[z, c]

    for piece in (0, 1):
        landed(sec_part(zl * 2 + o, piece), sc_s.at[12 + piece], sc_r.at[12 + piece])
        for hop in (1, 2):
            for side in (0, 1):
                at = sec_index(side, hop, piece)
                landed(sec_part(sec_node(side, hop) + o, piece), sc_s.at[at], sc_r.at[at])
        at = sec_index(piece, 3, piece)
        landed(sec_part(sec_node(piece, 3) + o, piece), sc_s.at[at], sc_r.at[at])

    for t in range(256):
        parts = []
        for n in range(12):
            first = 342 * n // 16
            if 342 * n < 16 * t + 16 and 342 * n + 342 > 16 * t:
                parts.append(wst[n, 16 * (t - first):16 * (t - first) + 16])
        tile = parts[0] if len(parts) == 1 else (parts[0].astype(F32) + parts[1].astype(F32)).astype(BF)
        wn[16 * t:16 * t + 16] = tile
    for i in range(8):
        igrad[:, 512 * i:512 * i + 512] = lax.dot_general(
            cot[...], wn[512 * i:512 * i + 512], (((1,), (1,)), ((), ())), preferred_element_type=F32
        ).astype(BF)

    stores = [pltpu.make_async_copy(igrad, igrad_out, in_s.at[3])]
    stores[0].start()

    for piece in (0, 1):
        at = 16 + piece
        landed(pri_part(o, 0, 0, piece), pc_s.at[at], pc_r.at[at])
        at = 8 + piece
        landed(alt_part(o, 0, 0, piece), rc_s.at[at], rc_r.at[at])
        for side in (0, 1):
            for hop in (1, 2, 3):
                at = pri_cross_at(side, hop, piece)
                landed(pri_part(o, side, hop, piece), pc_s.at[at], pc_r.at[at])
            at = alt_cross_at(side, 1, piece)
            landed(alt_part(o, side, 1, piece), rc_s.at[at], rc_r.at[at])
        at = pri_cross_at(piece, 4, piece)
        landed(pri_part(o, piece, 4, piece), pc_s.at[at], pc_r.at[at])
        at = alt_cross_at(piece, 2, piece)
        landed(alt_part(o, piece, 2, piece), rc_s.at[at], rc_r.at[at])
    for core in (0, 1):
        total = None
        for r in range(NY):
            w = jnp.concatenate([wf0[core, r].reshape(SLAB, LANES), wf1[core, :, r].reshape(SLAB, LANES)], axis=1)
            part = dot(te[(y + r) % NY], w)
            total = part if total is None else total + part
        keys[:, HALF * core:HALF * core + HALF] = total.astype(BF)

    stores.append(pltpu.make_async_copy(keys, keys_out, in_s.at[4]))
    stores[1].start()

    for d, rel in z_partners:
        at = d * 2 + rel
        landed(qr.at[(z - d + NZ) % NZ, o if rel else c], gz_s.at[at], gz_r.at[at])
    total = qr[0].astype(F32)
    for zz in range(1, NZ):
        total = total + qr[zz].astype(F32)
    total = total.reshape(32, 128)
    k = iota((24, 32), 1)
    want = 4 * (k % 8) + 2 * (k // 16) + (k // 8) % 2 - 2 * c
    pick = jnp.where((k % 8 < 6) & (iota((24, 32), 0) == want), 1.0, 0.0)
    acc[...] = lax.dot_general(
        pick, total, (((1,), (0,)), ((), ())), preferred_element_type=F32, precision=lax.Precision.HIGHEST
    )
    scale = 1.0 / jnp.sqrt(F32(128 * NX * NY * NZ * 2))
    wgrad[...] = acc[:22] * scale

    for one in stores:
        one.wait()
    for one in sent:
        one.wait_send()


def local(tokens, cotangent, prim_values, prim_scales, sec_values, sec_scales):
    dma = pltpu.SemaphoreType.DMA
    vmem = pl.BlockSpec(memory_space=pltpu.VMEM)
    hbm = pl.BlockSpec(memory_space=pltpu.HBM)
    groups = [24, 4, 16, 18, 8, 8, 10, 12, 14, 8, 12, 8, 16, 4, 24]
    return pl.pallas_call(
        kernel,
        name="sharded_projection",
        out_shape=(
            jax.ShapeDtypeStruct((128, 512), BF),
            jax.ShapeDtypeStruct((128, 4096), BF),
            jax.ShapeDtypeStruct((22, 128), F32),
        ),
        in_specs=[hbm, hbm, vmem, vmem, hbm, vmem],
        out_specs=(hbm, hbm, vmem),
        scratch_shapes=[
            pltpu.VMEM((128, 4096), BF),
            pltpu.VMEM((128, 512), BF),
            pltpu.VMEM((342, 512), BF),
            pltpu.VMEM((128, 512), BF),
            pltpu.VMEM((128, 4096), BF),
            dma((5,)),
            pltpu.VMEM((NY, 128, SLAB), BF),
            pltpu.VMEM((2, NY, NX, ROWS, LANES), BF),
            pltpu.VMEM((2, NX, NY, ROWS, LANES), BF),
            pltpu.VMEM((12, SEC, 512), BF),
            pltpu.VMEM((NY, NX, ROWS, HALF), BF),
            pltpu.VMEM((NY, NX, ROWS, HALF), BF),
            pltpu.VMEM((NX, NY, ROWS, LANES), BF),
            pltpu.VMEM((NY, NX, ROWS, LANES), BF),
            pltpu.VMEM((2, 4, ROWS, LANES), BF),
            pltpu.VMEM((2, NY, ROWS, LANES), BF),
            pltpu.VMEM((NY, ROWS, LANES), BF),
            pltpu.VMEM((NY, ROWS, LANES), BF),
            pltpu.VMEM((2, 4, NX, ROWS, LANES), BF),
            pltpu.VMEM((NX, ROWS, LANES), BF),
            pltpu.VMEM((NX, ROWS, LANES), BF),
            pltpu.VMEM((2, 16, 128), BF),
            pltpu.VMEM((NZ, 2, 16, 128), BF),
            pltpu.VMEM((NZ, 2, 16, 128), BF),
            pltpu.VMEM((NZ, 2, 16, 128), BF),
            pltpu.VMEM((24, 128), F32),
            pltpu.VMEM((4096, 512), BF),
        ]
        + [dma((n,)) for n in groups for _ in (0, 1)],
        compiler_params=pltpu.CompilerParams(
            collective_id=0, has_side_effects=True, vmem_limit_bytes=60 * 2**20
        ),
    )(tokens, cotangent, prim_values, prim_scales.reshape(1, -1), sec_values, sec_scales)


def solution(mesh):
    return jax.shard_map(
        local,
        mesh=mesh,
        in_specs=(
            P(("dp", "node"), None),
            P(("dp", "node"), None),
            P(("dp", "node"), None),
            P(("dp", "node")),
            P("node", None),
            P("node"),
        ),
        out_specs=(P(("dp", "node"), None), P(("dp", "node"), None), P(("dp", "node"), None)),
        check_vma=False,
    )
```

```python
import jax
import jax.numpy as jnp
from jax import lax
from jax.experimental import pallas as pl
from jax.experimental.pallas import tpu as pltpu
from jax.sharding import PartitionSpec as P

MESH = pl.DeviceIdType.MESH
BF = jnp.bfloat16
F32 = jnp.float32

NX, NY, NZ = 4, 8, 12
ROWS = 144
HALF = 256
SLAB = NX * ROWS
CUT = 64
ROWS0 = 80
ROWS1 = 2 * ROWS - ROWS0
CUT1 = 96
LANES = 128
SEC = 368
SEC_A = 192
RING = (4, 3, 5, 2, 6, 1, 7, 0)
PLACE = {r: k for k, r in enumerate(RING)}


def iota(shape, axis):
    return lax.broadcasted_iota(jnp.int32, shape, axis)


def one_hot(hit):
    return jnp.where(hit, 1.0, 0.0).astype(BF)


def line_of(k, half):
    z, core, h, i = k // 32, (k // 16) % 2, (k // 8) % 2, k % 8
    return jnp.where((i < 6) & (h == half), 11 * z + 5 * core + i, -1)


def dot(a, b):
    return jnp.dot(a, b, preferred_element_type=F32)


def kernel(
    tok_in, cot_in, pv, ps, sv_in, sc, keys_out, igrad_out, wgrad,
    tok, cot, sv, keys, igrad, in_s,
    te, wf0, wf1, wst, gs, gr, gx0, gx1, xr1, xr2, gy, yr, g1r, hx, xr3, pz, pr, qz, qr, acc, wn,
    pz_s, pz_r, px_s, px_r, py_s, py_r, pc_s, pc_r, ru_s, ru_r, rx_s, rx_r, rc_s, rc_r,
    sz_s, sz_r, sc_s, sc_r,
    gc_s, gc_r, gx_s, gx_r, gy_s, gy_r, hy_s, hy_r, hx_s, hx_r, gz_s, gz_r,
):
    dp, nd = lax.axis_index("dp"), lax.axis_index("node")
    x, y, z, c = dp % 4, (dp // 4) % 8, (dp // 32) * 6 + nd // 2, nd % 2
    o = 1 - c
    zl = nd // 2

    def dev(dx=0, dy=0, dz=0, core=None):
        xx, yy, zz = (x + dx) % NX, (y + dy) % NY, (z + dz) % NZ
        return ((zz // 6) * 32 + yy * 4 + xx, (zz % 6) * 2 + (c if core is None else core))

    sent = []

    def copy(src, dst, ssem, rsem, target):
        return pltpu.make_async_remote_copy(
            src_ref=src, dst_ref=dst, send_sem=ssem, recv_sem=rsem,
            device_id=target, device_id_type=MESH,
        )

    def send(src, dst, ssem, rsem, target):
        one = copy(src, dst, ssem, rsem, target)
        one.start()
        sent.append(one)

    def landed(dst, ssem, rsem):
        copy(dst, dst, ssem, rsem, dev(core=o)).wait_recv()

    z_partners = [(d, rel) for d in range(NZ) for rel in (0, 1) if (d, rel) != (0, 0)]
    z_partners.sort(key=lambda t: -min(t[0], NZ - t[0]))

    loads = [
        pltpu.make_async_copy(src, dst, in_s.at[i])
        for i, (src, dst) in enumerate(((sv_in, sv), (tok_in, tok), (cot_in, cot)))
    ]
    for one in loads:
        one.start()

    barrier = pltpu.get_barrier_semaphore()
    count = 0
    for d, rel in z_partners:
        pl.semaphore_signal(barrier, inc=1, device_id=dev(dz=d, core=o if rel else c), device_id_type=MESH)
        count += 1
    for d in (1, 2, 6, 7):
        pl.semaphore_signal(barrier, inc=1, device_id=dev(dy=d), device_id_type=MESH)
        count += 1
    for d in range(1, NX):
        pl.semaphore_signal(barrier, inc=1, device_id=dev(dx=d), device_id_type=MESH)
        count += 1

    k = iota((32, 22), 0)
    want = 4 * (k % 8) + 2 * (k // 16) + (k // 8) % 2 - 2 * c
    hit = (k % 8 < 6) & (iota((32, 22), 1) == want)
    factor = jnp.sum(jnp.where(hit, ps[...], 0.0), axis=1, keepdims=True)
    pz[...] = (dot(one_hot(hit), pv[...]) * factor).astype(BF).reshape(2, 16, 128)

    loads[0].wait()
    hit = iota((SEC, 342), 1) == iota((SEC, 342), 0) - (6 * nd) % 16
    factor = jnp.sum(jnp.where(hit, sc[...][None, :], 0.0), axis=1, keepdims=True)
    wst[nd] = (dot(one_hot(hit), sv[...]) * factor).astype(BF)

    d = iota((1, SLAB), 1)
    xx = (d >= ROWS).astype(jnp.int32) + (d >= 2 * ROWS).astype(jnp.int32) + (d >= 3 * ROWS).astype(jnp.int32)
    j = d - ROWS * xx
    low = jnp.where(j < 66, 66 * xx + j, -100000)
    high = jnp.where((j >= 66) & (j < 132), 66 * xx + j - 66, -100000)
    loads[1].wait()
    loads[2].wait()
    for yy in range(NY):
        total = None
        for start, base in ((264 * yy, low), (2112 + 264 * yy, high)):
            a = start // 128 * 128
            wide = min(384, 4096 - a)
            sel = one_hot(iota((wide, SLAB), 0) == base + (start - a))
            part = dot(tok[:, a:a + wide], sel)
            total = part if total is None else total + part
        te[yy] = total.astype(BF)

    def grad(k, core):
        part = cot[:, pl.ds(pl.multiple_of(core * HALF, HALF), HALF)]
        rows = te[(y + RING[k]) % NY]
        out = lax.dot_general(rows, part, (((0,), (0,)), ((), ())), preferred_element_type=F32)
        return out.reshape(NX, ROWS, HALF)

    def give(k):
        gs[k] = grad(k, o).astype(BF)
        send(gs.at[k], gr.at[k], gc_s.at[k], gc_r.at[k], dev(core=o))

    pl.semaphore_wait(barrier, count)

    for d, rel in z_partners:
        to = o if rel else c
        at = d * 2 + rel
        send(pz.at[to], pr.at[z, c], pz_s.at[at], pz_r.at[at], dev(dz=d, core=to))
    pr[z, c] = pz[c]

    for k in (0, 1):
        give(k)

    def sec_part(n, piece):
        return wst.at[n, pl.ds(0, SEC_A)] if piece == 0 else wst.at[n, pl.ds(SEC_A, SEC - SEC_A)]

    def sec_node(side, hop):
        return ((zl - hop + 6) % 6 if side == 0 else (zl + hop) % 6) * 2

    def sec_index(side, hop, piece):
        return side * 6 + (hop - 1) * 2 + piece

    def sec_send(side, hop, piece):
        part = sec_part(sec_node(side, hop - 1) + c, piece)
        at = sec_index(side, hop, piece)
        send(part, part, sz_s.at[at], sz_r.at[at], dev(dz=1 if side == 0 else NZ - 1))

    def sec_cross(side, hop, piece):
        part = sec_part(sec_node(side, hop) + c, piece)
        at = sec_index(side, hop, piece) if hop else 12 + piece
        send(part, part, sc_s.at[at], sc_r.at[at], dev(core=o))

    def sec_arrive(hop, order):
        for side in (0, 1):
            piece = side ^ order
            at = sec_index(side, hop, piece)
            landed(sec_part(sec_node(side, hop) + c, piece), sz_s.at[at], sz_r.at[at])
            if hop == 1 or (hop == 2 and order == 0):
                sec_send(side, hop + 1, piece)
            sec_cross(side, hop, piece)

    for order in (0, 1):
        for side in (0, 1):
            sec_send(side, 1, side ^ order)
    for k in range(2, 8):
        give(k)

    def pri_part(core, side, hop, piece):
        return wf0.at[core, (NY - hop) % NY if side == 0 else hop, pl.ds(2 * piece, 2)]

    def pri_send(side, hop, piece):
        at = side * 8 + (hop - 1) * 2 + piece
        send(pri_part(c, side, hop - 1, piece), pri_part(c, side, hop, piece),
             py_s.at[at], py_r.at[at], dev(dy=1 if side == 0 else NY - 1))

    def pri_cross_at(side, hop, piece):
        return side * 8 + (hop - 1) * 2 + piece if hop else 16 + piece

    def pri_cross(side, hop, piece):
        part = pri_part(c, side, hop, piece)
        at = pri_cross_at(side, hop, piece)
        send(part, part, pc_s.at[at], pc_r.at[at], dev(core=o))

    def pri_arrive(hop, order):
        for side in (0, 1):
            piece = side ^ order
            at = side * 8 + (hop - 1) * 2 + piece
            landed(pri_part(c, side, hop, piece), py_s.at[at], py_r.at[at])
            if hop < 3 or (hop == 3 and order == 0):
                pri_send(side, hop + 1, piece)
            pri_cross(side, hop, piece)

    def pri_turn():
        for d in range(1, NX):
            landed(wf0.at[c, 0, (x - d + NX) % NX], px_s.at[d], px_r.at[d])
        for order in (0, 1):
            for side in (0, 1):
                pri_send(side, 1, side ^ order)
        for piece in (0, 1):
            pri_cross(0, 0, piece)

    def near_slot(side, far):
        r = NY - 1 - far if side == 0 else 1 + far
        if far < 3:
            return wf1.at[c, x, r]
        return wf1.at[c, x, r, pl.ds(0, CUT1) if side == 0 else pl.ds(CUT1, ROWS1 - CUT1)]

    def near_send(side, far):
        slot = near_slot(side, far)
        if far < 2:
            src = wf1.at[c, x, 0]
        elif far == 2:
            src = near_slot(side, 1)
        else:
            src = wf1.at[c, x, 6 if side == 0 else 2, pl.ds(0, CUT1) if side == 0 else pl.ds(CUT1, ROWS1 - CUT1)]
        at = side * 4 + far
        step = 2 if far in (1, 3) else 1
        send(src, slot, ru_s.at[at], ru_r.at[at], dev(dy=step if side == 0 else NY - step))

    def near_landed(side, far):
        at = side * 4 + far
        landed(near_slot(side, far), ru_s.at[at], ru_r.at[at])

    def alt_mid():
        for side in (0, 1):
            near_landed(side, 1)
            near_send(side, 3)
            near_send(side, 2)

    def alt_part(core, side, hop, piece):
        xx = (x - hop + NX) % NX if side == 0 else (x + hop) % NX
        return wf1.at[core, xx, pl.ds(4 * piece, 4)]

    def alt_send(side, hop, piece):
        part = alt_part(c, side, hop - 1, piece)
        at = side * 4 + (hop - 1) * 2 + piece
        send(part, part, rx_s.at[at], rx_r.at[at], dev(dx=1 if side == 0 else NX - 1))

    def alt_cross_at(side, hop, piece):
        return side * 4 + (hop - 1) * 2 + piece if hop else 8 + piece

    def alt_cross(side, hop, piece):
        part = alt_part(c, side, hop, piece)
        at = alt_cross_at(side, hop, piece)
        send(part, part, rc_s.at[at], rc_r.at[at], dev(core=o))

    def alt_arrive(hop, order):
        for side in (0, 1):
            piece = side ^ order
            at = side * 4 + (hop - 1) * 2 + piece
            landed(alt_part(c, side, hop, piece), rx_s.at[at], rx_r.at[at])
            if hop == 1 and order == 0:
                alt_send(side, 2, piece)
            alt_cross(side, hop, piece)

    def alt_turn():
        for far in (0, 2, 3):
            for side in (0, 1):
                near_landed(side, far)
        for order in (0, 1):
            for side in (0, 1):
                alt_send(side, 1, side ^ order)
        for piece in (0, 1):
            alt_cross(0, 0, piece)

    def x_send(side, stage, p):
        far = (x + 2) % NX
        near = (x + 1) % NX if side == 0 else (x + NX - 1) % NX
        src = gx0.at[far if stage == 0 else near, pl.ds(2 * p, 2)]
        dst = xr1.at[side, pl.ds(2 * (p // 2), 2)] if stage == 0 else xr2.at[side, pl.ds(2 * p, 2)]
        at = side * 6 + (p // 2 if stage == 0 else 2 + p)
        send(src, dst, gx_s.at[at], gx_r.at[at], dev(dx=1 if side == 0 else NX - 1))

    def x_turn(p):
        side = p % 2
        at = side * 6 + p // 2
        landed(xr1.at[side, pl.ds(2 * (p // 2), 2)], gx_s.at[at], gx_r.at[at])
        near = (x + 1) % NX if side == 0 else (x + NX - 1) % NX
        for i in (0, 1):
            gx0[near, 2 * p + i] = (
                gx0[near, 2 * p + i].astype(F32) + xr1[side, 2 * (p // 2) + i].astype(F32)
            ).astype(BF)
        x_send(side, 1, p)

    def y_at(side, hop, piece):
        return side * 8 + (hop - 1) * 2 + piece

    def y_send(side, hop, piece):
        src = gx1.at[PLACE[5 - hop if side == 0 else 3 + hop], pl.ds(2 * piece, 2)]
        at = y_at(side, hop, piece)
        send(src, g1r.at[side, hop - 1, pl.ds(2 * piece, 2)], hy_s.at[at], hy_r.at[at],
             dev(dy=1 if side == 0 else NY - 1))

    def y_turn(side, hop, piece):
        at = y_at(side, hop, piece)
        part = pl.ds(2 * piece, 2)
        landed(g1r.at[side, hop - 1, part], hy_s.at[at], hy_r.at[at])
        k = PLACE[4 - hop if side == 0 else 4 + hop]
        gx1[k, part] = (gx1[k, part].astype(F32) + g1r[side, hop - 1, part].astype(F32)).astype(BF)
        y_send(side, hop + 1, piece)

    def own_half(p):
        for k in (2 * p, 2 * p + 1):
            mine = grad(k, c)
            landed(gr.at[k], gc_s.at[k], gc_r.at[k])
            mine = (mine + gr[k].astype(F32)).astype(BF)
            gx0[:, k] = mine[:, :, :LANES]
            gx1[k] = mine[:, :, LANES:]
            if RING[k] == 4:
                y_send(0, 1, 0)
                y_send(1, 1, 1)
            if RING[k] == 3:
                y_send(0, 2, 1)
            if RING[k] == 5:
                y_send(1, 2, 0)
        side = p % 2
        x_send(side, 0, p)
        x_send(1 - side, 1, p)

    def pri_line():
        for d, rel in z_partners:
            at = d * 2 + rel
            landed(pr.at[(z - d + NZ) % NZ, o if rel else c], pz_s.at[at], pz_r.at[at])
        packets = pr[...].reshape(NZ * 32, 128)
        k = iota((1, NZ * 32), 1)
        r = iota((ROWS, NZ * 32), 0)
        slab = dot(one_hot(line_of(k, 0) == r), packets).astype(BF)
        wf1[c, x, 0, pl.ds(0, ROWS)] = dot(one_hot(line_of(k, 1) == r), packets).astype(BF)
        wf1[c, x, 0, pl.ds(ROWS, ROWS - ROWS0)] = slab[ROWS0:]
        wf0[c, 0, x] = slab[:ROWS0]
        for far in (1, 0):
            for side in (0, 1):
                near_send(side, far)
        for d in (2, 1, 3):
            own = wf0.at[c, 0, x]
            send(own, own, px_s.at[d], px_r.at[d], dev(dx=d))

    own_half(0)
    own_half(1)
    pri_line()
    own_half(2)
    own_half(3)
    sec_arrive(1, 0)
    pri_turn()
    y_turn(0, 1, 0)
    y_turn(1, 1, 1)
    x_turn(0)
    x_turn(1)
    alt_mid()
    sec_arrive(1, 1)
    for piece in (0, 1):
        sec_cross(0, 0, piece)
    y_turn(0, 2, 1)
    y_turn(1, 2, 0)
    x_turn(2)
    x_turn(3)
    pri_arrive(1, 0)
    alt_turn()
    y_turn(0, 2, 0)
    y_turn(1, 2, 1)
    sec_arrive(2, 0)
    pri_arrive(1, 1)
    y_turn(0, 3, 1)
    y_turn(1, 3, 0)
    pri_arrive(2, 0)
    y_turn(0, 3, 0)
    y_turn(1, 3, 1)

    def fold_send(side, far, r):
        at = side * 4 + far
        k = PLACE[r]
        step = 2 if far in (1, 3) else 1
        part = pl.ds(0, ROWS) if far < 3 else (pl.ds(0, CUT) if side == 0 else pl.ds(CUT, ROWS - CUT))
        send(gy.at[k, part], yr.at[at, part], gy_s.at[at], gy_r.at[at], dev(dy=step if side == 0 else NY - step))

    def fold_landed(side, far):
        at = side * 4 + far
        part = pl.ds(0, ROWS) if far < 3 else (pl.ds(0, CUT) if side == 0 else pl.ds(CUT, ROWS - CUT))
        landed(yr.at[at, part], gy_s.at[at], gy_r.at[at])

    for p in (0, 1, 2, 3):
        for side in (0, 1):
            at = side * 6 + 2 + p
            landed(xr2.at[side, pl.ds(2 * p, 2)], gx_s.at[at], gx_r.at[at])
        for k in (2 * p, 2 * p + 1):
            gy[k] = (gx0[x, k].astype(F32) + xr2[0, k].astype(F32) + xr2[1, k].astype(F32)).astype(BF)
            r = RING[k]
            if r == 4:
                fold_send(0, 3, 4)
                fold_send(1, 3, 4)
            elif r in (3, 5):
                fold_send(0 if r == 3 else 1, 2, r)
            elif r in (1, 7):
                fold_send(0 if r == 1 else 1, 0, r)
    pri_arrive(2, 1)
    sec_arrive(2, 1)
    alt_arrive(1, 0)

    for piece in (1, 0):
        for side in (0, 1):
            at = y_at(side, 4, piece)
            landed(g1r.at[side, 3, pl.ds(2 * piece, 2)], hy_s.at[at], hy_r.at[at])
    hx[...] = (gx1[PLACE[0]].astype(F32) + g1r[0, 3].astype(F32) + g1r[1, 3].astype(F32)).astype(BF)
    for d in (2, 1, 3):
        send(hx.at[(x + d) % NX], xr3.at[d], hx_s.at[d], hx_r.at[d], dev(dx=d))
    xr3[0] = hx[x]

    for side in (0, 1):
        fold_landed(side, 2)
        fold_landed(side, 3)
        k = PLACE[2 if side == 0 else 6]
        gy[k] = (gy[k].astype(F32) + yr[side * 4 + 2].astype(F32)).astype(BF)
        part = pl.ds(0, CUT) if side == 0 else pl.ds(CUT, ROWS - CUT)
        gy[k, part] = (gy[k, part].astype(F32) + yr[side * 4 + 3, part].astype(F32)).astype(BF)
        fold_send(side, 1, 2 if side == 0 else 6)
    pri_arrive(3, 0)
    sec_arrive(3, 0)
    alt_arrive(1, 1)
    pri_arrive(3, 1)
    alt_arrive(2, 0)
    pri_arrive(4, 0)

    line0 = gy[PLACE[0]].astype(F32)
    for far in (0, 1):
        for side in (0, 1):
            fold_landed(side, far)
            line0 = line0 + yr[side * 4 + far].astype(F32)
    for d in range(1, NX):
        landed(xr3.at[d], hx_s.at[d], hx_r.at[d])
    line1 = xr3[0].astype(F32)
    for d in range(1, NX):
        line1 = line1 + xr3[d].astype(F32)
    k = iota((NZ * 32, 1), 0)
    r = iota((NZ * 32, ROWS), 1)
    packets = dot(one_hot(line_of(k, 0) == r), line0.astype(BF)) + dot(one_hot(line_of(k, 1) == r), line1.astype(BF))
    qz[...] = packets.astype(BF).reshape(NZ, 2, 16, 128)
    for d, rel in z_partners:
        to = o if rel else c
        at = d * 2 + rel
        send(qz.at[(z + d) % NZ, to], qr.at[z, c], gz_s.at[at], gz_r.at[at], dev(dz=d, core=to))
    qr[z, c] = qz[z, c]

    for piece in (0, 1):
        landed(sec_part(zl * 2 + o, piece), sc_s.at[12 + piece], sc_r.at[12 + piece])
        for hop in (1, 2):
            for side in (0, 1):
                at = sec_index(side, hop, piece)
                landed(sec_part(sec_node(side, hop) + o, piece), sc_s.at[at], sc_r.at[at])
        at = sec_index(piece, 3, piece)
        landed(sec_part(sec_node(piece, 3) + o, piece), sc_s.at[at], sc_r.at[at])

    for t in range(256):
        parts = []
        for n in range(12):
            first = 342 * n // 16
            if 342 * n < 16 * t + 16 and 342 * n + 342 > 16 * t:
                parts.append(wst[n, 16 * (t - first):16 * (t - first) + 16])
        tile = parts[0] if len(parts) == 1 else (parts[0].astype(F32) + parts[1].astype(F32)).astype(BF)
        wn[16 * t:16 * t + 16] = tile
    for i in range(8):
        igrad[:, 512 * i:512 * i + 512] = lax.dot_general(
            cot[...], wn[512 * i:512 * i + 512], (((1,), (1,)), ((), ())), preferred_element_type=F32
        ).astype(BF)

    stores = [pltpu.make_async_copy(igrad, igrad_out, in_s.at[3])]
    stores[0].start()

    for piece in (0, 1):
        at = 16 + piece
        landed(pri_part(o, 0, 0, piece), pc_s.at[at], pc_r.at[at])
        at = 8 + piece
        landed(alt_part(o, 0, 0, piece), rc_s.at[at], rc_r.at[at])
        for side in (0, 1):
            for hop in (1, 2, 3):
                at = pri_cross_at(side, hop, piece)
                landed(pri_part(o, side, hop, piece), pc_s.at[at], pc_r.at[at])
            at = alt_cross_at(side, 1, piece)
            landed(alt_part(o, side, 1, piece), rc_s.at[at], rc_r.at[at])
        at = pri_cross_at(piece, 4, piece)
        landed(pri_part(o, piece, 4, piece), pc_s.at[at], pc_r.at[at])
        at = alt_cross_at(piece, 2, piece)
        landed(alt_part(o, piece, 2, piece), rc_s.at[at], rc_r.at[at])
    for core in (0, 1):
        total = None
        for r in range(NY):
            first = jnp.concatenate([wf0[core, r], wf1[core, :, r, pl.ds(ROWS, ROWS - ROWS0)]], axis=1)
            second = wf1[core, :, r, pl.ds(0, ROWS)]
            w = jnp.concatenate([first.reshape(SLAB, LANES), second.reshape(SLAB, LANES)], axis=1)
            part = dot(te[(y + r) % NY], w)
            total = part if total is None else total + part
        keys[:, HALF * core:HALF * core + HALF] = total.astype(BF)

    stores.append(pltpu.make_async_copy(keys, keys_out, in_s.at[4]))
    stores[1].start()

    for one in sent:
        one.wait_send()

    for d, rel in z_partners:
        at = d * 2 + rel
        landed(qr.at[(z - d + NZ) % NZ, o if rel else c], gz_s.at[at], gz_r.at[at])
    total = qr[0].astype(F32)
    for zz in range(1, NZ):
        total = total + qr[zz].astype(F32)
    total = total.reshape(32, 128)
    k = iota((24, 32), 1)
    want = 4 * (k % 8) + 2 * (k // 16) + (k // 8) % 2 - 2 * c
    pick = jnp.where((k % 8 < 6) & (iota((24, 32), 0) == want), 1.0, 0.0)
    acc[...] = lax.dot_general(
        pick, total, (((1,), (0,)), ((), ())), preferred_element_type=F32, precision=lax.Precision.HIGHEST
    )
    scale = 1.0 / jnp.sqrt(F32(128 * NX * NY * NZ * 2))
    wgrad[...] = acc[:22] * scale

    for one in stores:
        one.wait()


def hand_over(keys, igrad, wgrad, keys_out, igrad_out, wgrad_out, out_s):
    copies = [pltpu.make_async_copy(wgrad, wgrad_out, out_s.at[0])]
    copies.append(pltpu.make_async_copy(keys, keys_out, out_s.at[1]))
    for i in range(8):
        part = pl.ds(16 * i, 16)
        copies.append(pltpu.make_async_copy(igrad.at[part], igrad_out.at[part], out_s.at[2 + i]))
    for one in copies:
        one.start()
    for one in copies:
        one.wait()


def local(tokens, cotangent, prim_values, prim_scales, sec_values, sec_scales):
    dma = pltpu.SemaphoreType.DMA
    vmem = pl.BlockSpec(memory_space=pltpu.VMEM)
    hbm = pl.BlockSpec(memory_space=pltpu.HBM)
    groups = [24, 4, 16, 18, 8, 8, 10, 12, 14, 8, 12, 8, 16, 4, 24]
    shapes = (
        jax.ShapeDtypeStruct((128, 512), BF),
        jax.ShapeDtypeStruct((128, 4096), BF),
        jax.ShapeDtypeStruct((22, 128), F32),
    )
    results = pl.pallas_call(
        kernel,
        name="sharded_projection",
        out_shape=shapes,
        in_specs=[hbm, hbm, vmem, vmem, hbm, vmem],
        out_specs=(hbm, hbm, vmem),
        scratch_shapes=[
            pltpu.VMEM((128, 4096), BF),
            pltpu.VMEM((128, 512), BF),
            pltpu.VMEM((342, 512), BF),
            pltpu.VMEM((128, 512), BF),
            pltpu.VMEM((128, 4096), BF),
            dma((5,)),
            pltpu.VMEM((NY, 128, SLAB), BF),
            pltpu.VMEM((2, NY, NX, ROWS0, LANES), BF),
            pltpu.VMEM((2, NX, NY, ROWS1, LANES), BF),
            pltpu.VMEM((12, SEC, 512), BF),
            pltpu.VMEM((NY, NX, ROWS, HALF), BF),
            pltpu.VMEM((NY, NX, ROWS, HALF), BF),
            pltpu.VMEM((NX, NY, ROWS, LANES), BF),
            pltpu.VMEM((NY, NX, ROWS, LANES), BF),
            pltpu.VMEM((2, 4, ROWS, LANES), BF),
            pltpu.VMEM((2, NY, ROWS, LANES), BF),
            pltpu.VMEM((NY, ROWS, LANES), BF),
            pltpu.VMEM((NY, ROWS, LANES), BF),
            pltpu.VMEM((2, 4, NX, ROWS, LANES), BF),
            pltpu.VMEM((NX, ROWS, LANES), BF),
            pltpu.VMEM((NX, ROWS, LANES), BF),
            pltpu.VMEM((2, 16, 128), BF),
            pltpu.VMEM((NZ, 2, 16, 128), BF),
            pltpu.VMEM((NZ, 2, 16, 128), BF),
            pltpu.VMEM((NZ, 2, 16, 128), BF),
            pltpu.VMEM((24, 128), F32),
            pltpu.VMEM((4096, 512), BF),
        ]
        + [dma((n,)) for n in groups for _ in (0, 1)],
        compiler_params=pltpu.CompilerParams(
            collective_id=0, has_side_effects=True, vmem_limit_bytes=60 * 2**20
        ),
    )(tokens, cotangent, prim_values, prim_scales.reshape(1, -1), sec_values, sec_scales)
    return pl.pallas_call(
        hand_over,
        name="results",
        out_shape=shapes,
        in_specs=[hbm] * 3,
        out_specs=(hbm, hbm, hbm),
        scratch_shapes=[dma((10,))],
        compiler_params=pltpu.CompilerParams(vmem_limit_bytes=60 * 2**20),
    )(*results)


def solution(mesh):
    return jax.shard_map(
        local,
        mesh=mesh,
        in_specs=(
            P(("dp", "node"), None),
            P(("dp", "node"), None),
            P(("dp", "node"), None),
            P(("dp", "node")),
            P("node", None),
            P("node"),
        ),
        out_specs=(P(("dp", "node"), None), P(("dp", "node"), None), P(("dp", "node"), None)),
        check_vma=False,
    )
```

```python
import jax
import jax.numpy as jnp
from jax import lax
from jax.experimental import pallas as pl
from jax.experimental.pallas import tpu as pltpu
from jax.sharding import PartitionSpec as P

MESH = pl.DeviceIdType.MESH
BF = jnp.bfloat16
F32 = jnp.float32

NX, NY, NZ = 4, 8, 12
ROWS = 144
HALF = 256
SLAB = NX * ROWS
CUT = 64
ROWS0 = 80
ROWS1 = 2 * ROWS - ROWS0
CUT1 = 96
LANES = 128
SEC = 368
SEC_A = 192
RING = (4, 3, 5, 2, 6, 1, 7, 0)
PLACE = {r: k for k, r in enumerate(RING)}


def iota(shape, axis):
    return lax.broadcasted_iota(jnp.int32, shape, axis)


def one_hot(hit):
    return jnp.where(hit, 1.0, 0.0).astype(BF)


def line_of(k, half):
    z, core, h, i = k // 32, (k // 16) % 2, (k // 8) % 2, k % 8
    return jnp.where((i < 6) & (h == half), 11 * z + 5 * core + i, -1)


def dot(a, b):
    return jnp.dot(a, b, preferred_element_type=F32)


def kernel(
    tok_in, cot_in, pv, ps, sv_in, sc, keys_out, igrad_out, wgrad,
    tok, cot, sv, keys, igrad, in_s,
    te, wf0, wf1, wst, gs, gr, gx0, gx1, xr1, xr2, gy, yr, g1r, hx, xr3, pz, pr, qz, qr, acc, wn,
    pz_s, pz_r, px_s, px_r, py_s, py_r, pc_s, pc_r, ru_s, ru_r, rx_s, rx_r, rc_s, rc_r,
    sz_s, sz_r, sc_s, sc_r,
    gc_s, gc_r, gx_s, gx_r, gy_s, gy_r, hy_s, hy_r, hx_s, hx_r, gz_s, gz_r,
):
    dp, nd = lax.axis_index("dp"), lax.axis_index("node")
    x, y, z, c = dp % 4, (dp // 4) % 8, (dp // 32) * 6 + nd // 2, nd % 2
    o = 1 - c
    zl = nd // 2

    def dev(dx=0, dy=0, dz=0, core=None):
        xx, yy, zz = (x + dx) % NX, (y + dy) % NY, (z + dz) % NZ
        return ((zz // 6) * 32 + yy * 4 + xx, (zz % 6) * 2 + (c if core is None else core))

    sent = []

    def copy(src, dst, ssem, rsem, target):
        return pltpu.make_async_remote_copy(
            src_ref=src, dst_ref=dst, send_sem=ssem, recv_sem=rsem,
            device_id=target, device_id_type=MESH,
        )

    def send(src, dst, ssem, rsem, target):
        one = copy(src, dst, ssem, rsem, target)
        one.start()
        sent.append(one)

    def landed(dst, ssem, rsem):
        copy(dst, dst, ssem, rsem, dev(core=o)).wait_recv()

    z_partners = [(d, rel) for d in range(NZ) for rel in (0, 1) if (d, rel) != (0, 0)]
    z_partners.sort(key=lambda t: -min(t[0], NZ - t[0]))

    loads = [
        pltpu.make_async_copy(src, dst, in_s.at[i])
        for i, (src, dst) in enumerate(((sv_in, sv), (tok_in, tok), (cot_in, cot)))
    ]
    for one in loads:
        one.start()

    barrier = pltpu.get_barrier_semaphore()
    count = 0
    for d, rel in z_partners:
        pl.semaphore_signal(barrier, inc=1, device_id=dev(dz=d, core=o if rel else c), device_id_type=MESH)
        count += 1
    for d in (1, 2, 6, 7):
        pl.semaphore_signal(barrier, inc=1, device_id=dev(dy=d), device_id_type=MESH)
        count += 1
    for d in range(1, NX):
        pl.semaphore_signal(barrier, inc=1, device_id=dev(dx=d), device_id_type=MESH)
        count += 1

    k = iota((32, 22), 0)
    want = 4 * (k % 8) + 2 * (k // 16) + (k // 8) % 2 - 2 * c
    hit = (k % 8 < 6) & (iota((32, 22), 1) == want)
    factor = jnp.sum(jnp.where(hit, ps[...], 0.0), axis=1, keepdims=True)
    pz[...] = (dot(one_hot(hit), pv[...]) * factor).astype(BF).reshape(2, 16, 128)

    loads[0].wait()
    hit = iota((SEC, 342), 1) == iota((SEC, 342), 0) - (6 * nd) % 16
    factor = jnp.sum(jnp.where(hit, sc[...][None, :], 0.0), axis=1, keepdims=True)
    wst[nd] = (dot(one_hot(hit), sv[...]) * factor).astype(BF)

    d = iota((1, SLAB), 1)
    xx = (d >= ROWS).astype(jnp.int32) + (d >= 2 * ROWS).astype(jnp.int32) + (d >= 3 * ROWS).astype(jnp.int32)
    j = d - ROWS * xx
    low = jnp.where(j < 66, 66 * xx + j, -100000)
    high = jnp.where((j >= 66) & (j < 132), 66 * xx + j - 66, -100000)
    loads[1].wait()
    loads[2].wait()
    for yy in range(NY):
        total = None
        for start, base in ((264 * yy, low), (2112 + 264 * yy, high)):
            a = start // 128 * 128
            wide = min(384, 4096 - a)
            sel = one_hot(iota((wide, SLAB), 0) == base + (start - a))
            part = dot(tok[:, a:a + wide], sel)
            total = part if total is None else total + part
        te[yy] = total.astype(BF)

    def grad(k, core):
        part = cot[:, pl.ds(pl.multiple_of(core * HALF, HALF), HALF)]
        rows = te[(y + RING[k]) % NY]
        out = lax.dot_general(rows, part, (((0,), (0,)), ((), ())), preferred_element_type=F32)
        return out.reshape(NX, ROWS, HALF)

    def give(k):
        gs[k] = grad(k, o).astype(BF)
        send(gs.at[k], gr.at[k], gc_s.at[k], gc_r.at[k], dev(core=o))

    pl.semaphore_wait(barrier, count)

    for d, rel in z_partners:
        to = o if rel else c
        at = d * 2 + rel
        send(pz.at[to], pr.at[z, c], pz_s.at[at], pz_r.at[at], dev(dz=d, core=to))
    pr[z, c] = pz[c]

    for k in (0, 1):
        give(k)

    def sec_part(n, piece):
        return wst.at[n, pl.ds(0, SEC_A)] if piece == 0 else wst.at[n, pl.ds(SEC_A, SEC - SEC_A)]

    def sec_node(side, hop):
        return ((zl - hop + 6) % 6 if side == 0 else (zl + hop) % 6) * 2

    def sec_index(side, hop, piece):
        return side * 6 + (hop - 1) * 2 + piece

    def sec_send(side, hop, piece):
        part = sec_part(sec_node(side, hop - 1) + c, piece)
        at = sec_index(side, hop, piece)
        send(part, part, sz_s.at[at], sz_r.at[at], dev(dz=1 if side == 0 else NZ - 1))

    def sec_cross(side, hop, piece):
        part = sec_part(sec_node(side, hop) + c, piece)
        at = sec_index(side, hop, piece) if hop else 12 + piece
        send(part, part, sc_s.at[at], sc_r.at[at], dev(core=o))

    def sec_arrive(hop, order):
        for side in (0, 1):
            piece = side ^ order
            at = sec_index(side, hop, piece)
            landed(sec_part(sec_node(side, hop) + c, piece), sz_s.at[at], sz_r.at[at])
            if hop == 1 or (hop == 2 and order == 0):
                sec_send(side, hop + 1, piece)
            sec_cross(side, hop, piece)

    for order in (0, 1):
        for side in (0, 1):
            sec_send(side, 1, side ^ order)
    for k in range(2, 8):
        give(k)

    def pri_part(core, side, hop, piece):
        return wf0.at[core, (NY - hop) % NY if side == 0 else hop, pl.ds(2 * piece, 2)]

    def pri_send(side, hop, piece):
        at = side * 8 + (hop - 1) * 2 + piece
        send(pri_part(c, side, hop - 1, piece), pri_part(c, side, hop, piece),
             py_s.at[at], py_r.at[at], dev(dy=1 if side == 0 else NY - 1))

    def pri_cross_at(side, hop, piece):
        return side * 8 + (hop - 1) * 2 + piece if hop else 16 + piece

    def pri_cross(side, hop, piece):
        part = pri_part(c, side, hop, piece)
        at = pri_cross_at(side, hop, piece)
        send(part, part, pc_s.at[at], pc_r.at[at], dev(core=o))

    def pri_arrive(hop, order):
        for side in (0, 1):
            piece = side ^ order
            at = side * 8 + (hop - 1) * 2 + piece
            landed(pri_part(c, side, hop, piece), py_s.at[at], py_r.at[at])
            if hop < 3 or (hop == 3 and order == 0):
                pri_send(side, hop + 1, piece)
            pri_cross(side, hop, piece)

    def pri_turn():
        for d in range(1, NX):
            landed(wf0.at[c, 0, (x - d + NX) % NX], px_s.at[d], px_r.at[d])
        for order in (0, 1):
            for side in (0, 1):
                pri_send(side, 1, side ^ order)
        for piece in (0, 1):
            pri_cross(0, 0, piece)

    def near_slot(side, far):
        r = NY - 1 - far if side == 0 else 1 + far
        if far < 3:
            return wf1.at[c, x, r]
        return wf1.at[c, x, r, pl.ds(0, CUT1) if side == 0 else pl.ds(CUT1, ROWS1 - CUT1)]

    def near_send(side, far):
        slot = near_slot(side, far)
        if far < 2:
            src = wf1.at[c, x, 0]
        elif far == 2:
            src = near_slot(side, 1)
        else:
            src = wf1.at[c, x, 6 if side == 0 else 2, pl.ds(0, CUT1) if side == 0 else pl.ds(CUT1, ROWS1 - CUT1)]
        at = side * 4 + far
        step = 2 if far in (1, 3) else 1
        send(src, slot, ru_s.at[at], ru_r.at[at], dev(dy=step if side == 0 else NY - step))

    def near_landed(side, far):
        at = side * 4 + far
        landed(near_slot(side, far), ru_s.at[at], ru_r.at[at])

    def alt_mid():
        for side in (0, 1):
            near_landed(side, 1)
            near_send(side, 3)
            near_send(side, 2)

    def alt_part(core, side, hop, piece):
        xx = (x - hop + NX) % NX if side == 0 else (x + hop) % NX
        return wf1.at[core, xx, pl.ds(4 * piece, 4)]

    def alt_send(side, hop, piece):
        part = alt_part(c, side, hop - 1, piece)
        at = side * 4 + (hop - 1) * 2 + piece
        send(part, part, rx_s.at[at], rx_r.at[at], dev(dx=1 if side == 0 else NX - 1))

    def alt_cross_at(side, hop, piece):
        return side * 4 + (hop - 1) * 2 + piece if hop else 8 + piece

    def alt_cross(side, hop, piece):
        part = alt_part(c, side, hop, piece)
        at = alt_cross_at(side, hop, piece)
        send(part, part, rc_s.at[at], rc_r.at[at], dev(core=o))

    def alt_arrive(hop, order):
        for side in (0, 1):
            piece = side ^ order
            at = side * 4 + (hop - 1) * 2 + piece
            landed(alt_part(c, side, hop, piece), rx_s.at[at], rx_r.at[at])
            if hop == 1 and order == 0:
                alt_send(side, 2, piece)
            alt_cross(side, hop, piece)

    def alt_turn():
        for far in (0, 2, 3):
            for side in (0, 1):
                near_landed(side, far)
        for order in (0, 1):
            for side in (0, 1):
                alt_send(side, 1, side ^ order)
        for piece in (0, 1):
            alt_cross(0, 0, piece)

    def x_send(side, stage, p):
        far = (x + 2) % NX
        near = (x + 1) % NX if side == 0 else (x + NX - 1) % NX
        src = gx0.at[far if stage == 0 else near, pl.ds(2 * p, 2)]
        dst = xr1.at[side, pl.ds(2 * (p // 2), 2)] if stage == 0 else xr2.at[side, pl.ds(2 * p, 2)]
        at = side * 6 + (p // 2 if stage == 0 else 2 + p)
        send(src, dst, gx_s.at[at], gx_r.at[at], dev(dx=1 if side == 0 else NX - 1))

    def x_turn(p):
        side = p % 2
        at = side * 6 + p // 2
        landed(xr1.at[side, pl.ds(2 * (p // 2), 2)], gx_s.at[at], gx_r.at[at])
        near = (x + 1) % NX if side == 0 else (x + NX - 1) % NX
        for i in (0, 1):
            gx0[near, 2 * p + i] = (
                gx0[near, 2 * p + i].astype(F32) + xr1[side, 2 * (p // 2) + i].astype(F32)
            ).astype(BF)
        x_send(side, 1, p)

    def y_at(side, hop, piece):
        return side * 8 + (hop - 1) * 2 + piece

    def y_send(side, hop, piece):
        src = gx1.at[PLACE[5 - hop if side == 0 else 3 + hop], pl.ds(2 * piece, 2)]
        at = y_at(side, hop, piece)
        send(src, g1r.at[side, hop - 1, pl.ds(2 * piece, 2)], hy_s.at[at], hy_r.at[at],
             dev(dy=1 if side == 0 else NY - 1))

    def y_turn(side, hop, piece):
        at = y_at(side, hop, piece)
        part = pl.ds(2 * piece, 2)
        landed(g1r.at[side, hop - 1, part], hy_s.at[at], hy_r.at[at])
        k = PLACE[4 - hop if side == 0 else 4 + hop]
        gx1[k, part] = (gx1[k, part].astype(F32) + g1r[side, hop - 1, part].astype(F32)).astype(BF)
        y_send(side, hop + 1, piece)

    def own_half(p):
        for k in (2 * p, 2 * p + 1):
            mine = grad(k, c)
            landed(gr.at[k], gc_s.at[k], gc_r.at[k])
            mine = (mine + gr[k].astype(F32)).astype(BF)
            gx0[:, k] = mine[:, :, :LANES]
            gx1[k] = mine[:, :, LANES:]
            if RING[k] == 4:
                y_send(0, 1, 0)
                y_send(1, 1, 1)
            if RING[k] == 3:
                y_send(0, 2, 1)
            if RING[k] == 5:
                y_send(1, 2, 0)
        side = p % 2
        x_send(side, 0, p)
        x_send(1 - side, 1, p)

    def pri_line():
        for d, rel in z_partners:
            at = d * 2 + rel
            landed(pr.at[(z - d + NZ) % NZ, o if rel else c], pz_s.at[at], pz_r.at[at])
        packets = pr[...].reshape(NZ * 32, 128)
        k = iota((1, NZ * 32), 1)
        r = iota((ROWS, NZ * 32), 0)
        slab = dot(one_hot(line_of(k, 0) == r), packets).astype(BF)
        wf1[c, x, 0, pl.ds(0, ROWS)] = dot(one_hot(line_of(k, 1) == r), packets).astype(BF)
        wf1[c, x, 0, pl.ds(ROWS, ROWS - ROWS0)] = slab[ROWS0:]
        wf0[c, 0, x] = slab[:ROWS0]
        for far in (1, 0):
            for side in (0, 1):
                near_send(side, far)
        for d in (2, 1, 3):
            own = wf0.at[c, 0, x]
            send(own, own, px_s.at[d], px_r.at[d], dev(dx=d))

    own_half(0)
    own_half(1)
    pri_line()
    own_half(2)
    own_half(3)
    sec_arrive(1, 0)
    pri_turn()
    y_turn(0, 1, 0)
    y_turn(1, 1, 1)
    x_turn(0)
    x_turn(1)
    alt_mid()
    sec_arrive(1, 1)
    for piece in (0, 1):
        sec_cross(0, 0, piece)
    y_turn(0, 2, 1)
    y_turn(1, 2, 0)
    x_turn(2)
    x_turn(3)
    pri_arrive(1, 0)
    alt_turn()
    y_turn(0, 2, 0)
    y_turn(1, 2, 1)
    sec_arrive(2, 0)
    pri_arrive(1, 1)
    def fold_send(side, far, r):
        at = side * 4 + far
        k = PLACE[r]
        step = 2 if far in (1, 3) else 1
        part = pl.ds(0, ROWS) if far < 3 else (pl.ds(0, CUT) if side == 0 else pl.ds(CUT, ROWS - CUT))
        send(gy.at[k, part], yr.at[at, part], gy_s.at[at], gy_r.at[at], dev(dy=step if side == 0 else NY - step))

    def fold_landed(side, far):
        at = side * 4 + far
        part = pl.ds(0, ROWS) if far < 3 else (pl.ds(0, CUT) if side == 0 else pl.ds(CUT, ROWS - CUT))
        landed(yr.at[at, part], gy_s.at[at], gy_r.at[at])

    for p in (0, 1, 2, 3):
        for side in (0, 1):
            at = side * 6 + 2 + p
            landed(xr2.at[side, pl.ds(2 * p, 2)], gx_s.at[at], gx_r.at[at])
        for k in (2 * p, 2 * p + 1):
            gy[k] = (gx0[x, k].astype(F32) + xr2[0, k].astype(F32) + xr2[1, k].astype(F32)).astype(BF)
            r = RING[k]
            if r == 4:
                fold_send(0, 3, 4)
                fold_send(1, 3, 4)
            elif r in (3, 5):
                fold_send(0 if r == 3 else 1, 2, r)
            elif r in (1, 7):
                fold_send(0 if r == 1 else 1, 0, r)
    y_turn(0, 3, 1)
    y_turn(1, 3, 0)
    pri_arrive(2, 0)
    y_turn(0, 3, 0)
    y_turn(1, 3, 1)

    for side in (0, 1):
        fold_landed(side, 2)
        fold_landed(side, 3)
        k = PLACE[2 if side == 0 else 6]
        gy[k] = (gy[k].astype(F32) + yr[side * 4 + 2].astype(F32)).astype(BF)
        part = pl.ds(0, CUT) if side == 0 else pl.ds(CUT, ROWS - CUT)
        gy[k, part] = (gy[k, part].astype(F32) + yr[side * 4 + 3, part].astype(F32)).astype(BF)
        fold_send(side, 1, 2 if side == 0 else 6)

    pri_arrive(2, 1)
    sec_arrive(2, 1)
    alt_arrive(1, 0)

    for piece in (1, 0):
        for side in (0, 1):
            at = y_at(side, 4, piece)
            landed(g1r.at[side, 3, pl.ds(2 * piece, 2)], hy_s.at[at], hy_r.at[at])
    hx[...] = (gx1[PLACE[0]].astype(F32) + g1r[0, 3].astype(F32) + g1r[1, 3].astype(F32)).astype(BF)
    for d in (2, 1, 3):
        send(hx.at[(x + d) % NX], xr3.at[d], hx_s.at[d], hx_r.at[d], dev(dx=d))
    xr3[0] = hx[x]

    pri_arrive(3, 0)

    line0 = gy[PLACE[0]].astype(F32)
    for far in (0, 1):
        for side in (0, 1):
            fold_landed(side, far)
            line0 = line0 + yr[side * 4 + far].astype(F32)
    for d in range(1, NX):
        landed(xr3.at[d], hx_s.at[d], hx_r.at[d])
    line1 = xr3[0].astype(F32)
    for d in range(1, NX):
        line1 = line1 + xr3[d].astype(F32)
    k = iota((NZ * 32, 1), 0)
    r = iota((NZ * 32, ROWS), 1)
    packets = dot(one_hot(line_of(k, 0) == r), line0.astype(BF)) + dot(one_hot(line_of(k, 1) == r), line1.astype(BF))
    qz[...] = packets.astype(BF).reshape(NZ, 2, 16, 128)
    for d, rel in z_partners:
        to = o if rel else c
        at = d * 2 + rel
        send(qz.at[(z + d) % NZ, to], qr.at[z, c], gz_s.at[at], gz_r.at[at], dev(dz=d, core=to))
    qr[z, c] = qz[z, c]

    sec_arrive(3, 0)
    alt_arrive(1, 1)
    pri_arrive(3, 1)
    alt_arrive(2, 0)
    pri_arrive(4, 0)

    for piece in (0, 1):
        landed(sec_part(zl * 2 + o, piece), sc_s.at[12 + piece], sc_r.at[12 + piece])
        for hop in (1, 2):
            for side in (0, 1):
                at = sec_index(side, hop, piece)
                landed(sec_part(sec_node(side, hop) + o, piece), sc_s.at[at], sc_r.at[at])
        at = sec_index(piece, 3, piece)
        landed(sec_part(sec_node(piece, 3) + o, piece), sc_s.at[at], sc_r.at[at])

    for t in range(256):
        parts = []
        for n in range(12):
            first = 342 * n // 16
            if 342 * n < 16 * t + 16 and 342 * n + 342 > 16 * t:
                parts.append(wst[n, 16 * (t - first):16 * (t - first) + 16])
        tile = parts[0] if len(parts) == 1 else (parts[0].astype(F32) + parts[1].astype(F32)).astype(BF)
        wn[16 * t:16 * t + 16] = tile
    for i in range(8):
        igrad[:, 512 * i:512 * i + 512] = lax.dot_general(
            cot[...], wn[512 * i:512 * i + 512], (((1,), (1,)), ((), ())), preferred_element_type=F32
        ).astype(BF)

    stores = [pltpu.make_async_copy(igrad, igrad_out, in_s.at[3])]
    stores[0].start()

    for piece in (0, 1):
        at = 16 + piece
        landed(pri_part(o, 0, 0, piece), pc_s.at[at], pc_r.at[at])
        at = 8 + piece
        landed(alt_part(o, 0, 0, piece), rc_s.at[at], rc_r.at[at])
        for side in (0, 1):
            for hop in (1, 2, 3):
                at = pri_cross_at(side, hop, piece)
                landed(pri_part(o, side, hop, piece), pc_s.at[at], pc_r.at[at])
            at = alt_cross_at(side, 1, piece)
            landed(alt_part(o, side, 1, piece), rc_s.at[at], rc_r.at[at])
        at = pri_cross_at(piece, 4, piece)
        landed(pri_part(o, piece, 4, piece), pc_s.at[at], pc_r.at[at])
        at = alt_cross_at(piece, 2, piece)
        landed(alt_part(o, piece, 2, piece), rc_s.at[at], rc_r.at[at])
    for core in (0, 1):
        total = None
        for r in range(NY):
            first = jnp.concatenate([wf0[core, r], wf1[core, :, r, pl.ds(ROWS, ROWS - ROWS0)]], axis=1)
            second = wf1[core, :, r, pl.ds(0, ROWS)]
            w = jnp.concatenate([first.reshape(SLAB, LANES), second.reshape(SLAB, LANES)], axis=1)
            part = dot(te[(y + r) % NY], w)
            total = part if total is None else total + part
        keys[:, HALF * core:HALF * core + HALF] = total.astype(BF)

    stores.append(pltpu.make_async_copy(keys, keys_out, in_s.at[4]))
    stores[1].start()

    for one in sent:
        one.wait_send()

    for d, rel in z_partners:
        at = d * 2 + rel
        landed(qr.at[(z - d + NZ) % NZ, o if rel else c], gz_s.at[at], gz_r.at[at])
    total = qr[0].astype(F32)
    for zz in range(1, NZ):
        total = total + qr[zz].astype(F32)
    total = total.reshape(32, 128)
    k = iota((24, 32), 1)
    want = 4 * (k % 8) + 2 * (k // 16) + (k // 8) % 2 - 2 * c
    pick = jnp.where((k % 8 < 6) & (iota((24, 32), 0) == want), 1.0, 0.0)
    acc[...] = lax.dot_general(
        pick, total, (((1,), (0,)), ((), ())), preferred_element_type=F32, precision=lax.Precision.HIGHEST
    )
    scale = 1.0 / jnp.sqrt(F32(128 * NX * NY * NZ * 2))
    wgrad[...] = acc[:22] * scale

    for one in stores:
        one.wait()


def hand_over(keys, igrad, wgrad, keys_out, igrad_out, wgrad_out, keys_at, igrad_at, wgrad_at, in_s, out_s):
    moves = [(keys, keys_at, keys_out), (wgrad, wgrad_at, wgrad_out)]
    for i in range(4):
        part = pl.ds(32 * i, 32)
        moves.append((igrad.at[part], igrad_at.at[part], igrad_out.at[part]))
    loads = [pltpu.make_async_copy(src, mid, in_s.at[i]) for i, (src, mid, dst) in enumerate(moves)]
    stores = [pltpu.make_async_copy(mid, dst, out_s.at[i]) for i, (src, mid, dst) in enumerate(moves)]
    for one in loads:
        one.start()
    for load, store in zip(loads, stores):
        load.wait()
        store.start()
    for one in stores:
        one.wait()


def local(tokens, cotangent, prim_values, prim_scales, sec_values, sec_scales):
    dma = pltpu.SemaphoreType.DMA
    vmem = pl.BlockSpec(memory_space=pltpu.VMEM)
    hbm = pl.BlockSpec(memory_space=pltpu.HBM)
    groups = [24, 4, 16, 18, 8, 8, 10, 12, 14, 8, 12, 8, 16, 4, 24]
    shapes = (
        jax.ShapeDtypeStruct((128, 512), BF),
        jax.ShapeDtypeStruct((128, 4096), BF),
        jax.ShapeDtypeStruct((22, 128), F32),
    )
    results = pl.pallas_call(
        kernel,
        name="sharded_projection",
        out_shape=shapes,
        in_specs=[hbm, hbm, vmem, vmem, hbm, vmem],
        out_specs=(hbm, hbm, vmem),
        scratch_shapes=[
            pltpu.VMEM((128, 4096), BF),
            pltpu.VMEM((128, 512), BF),
            pltpu.VMEM((342, 512), BF),
            pltpu.VMEM((128, 512), BF),
            pltpu.VMEM((128, 4096), BF),
            dma((5,)),
            pltpu.VMEM((NY, 128, SLAB), BF),
            pltpu.VMEM((2, NY, NX, ROWS0, LANES), BF),
            pltpu.VMEM((2, NX, NY, ROWS1, LANES), BF),
            pltpu.VMEM((12, SEC, 512), BF),
            pltpu.VMEM((NY, NX, ROWS, HALF), BF),
            pltpu.VMEM((NY, NX, ROWS, HALF), BF),
            pltpu.VMEM((NX, NY, ROWS, LANES), BF),
            pltpu.VMEM((NY, NX, ROWS, LANES), BF),
            pltpu.VMEM((2, 4, ROWS, LANES), BF),
            pltpu.VMEM((2, NY, ROWS, LANES), BF),
            pltpu.VMEM((NY, ROWS, LANES), BF),
            pltpu.VMEM((NY, ROWS, LANES), BF),
            pltpu.VMEM((2, 4, NX, ROWS, LANES), BF),
            pltpu.VMEM((NX, ROWS, LANES), BF),
            pltpu.VMEM((NX, ROWS, LANES), BF),
            pltpu.VMEM((2, 16, 128), BF),
            pltpu.VMEM((NZ, 2, 16, 128), BF),
            pltpu.VMEM((NZ, 2, 16, 128), BF),
            pltpu.VMEM((NZ, 2, 16, 128), BF),
            pltpu.VMEM((24, 128), F32),
            pltpu.VMEM((4096, 512), BF),
        ]
        + [dma((n,)) for n in groups for _ in (0, 1)],
        compiler_params=pltpu.CompilerParams(
            collective_id=0, has_side_effects=True, vmem_limit_bytes=60 * 2**20
        ),
    )(tokens, cotangent, prim_values, prim_scales.reshape(1, -1), sec_values, sec_scales)
    return pl.pallas_call(
        hand_over,
        name="results",
        out_shape=shapes,
        in_specs=[hbm] * 3,
        out_specs=(hbm, hbm, hbm),
        scratch_shapes=[
            pltpu.VMEM((128, 512), BF),
            pltpu.VMEM((128, 4096), BF),
            pltpu.VMEM((22, 128), F32),
            dma((6,)),
            dma((6,)),
        ],
        compiler_params=pltpu.CompilerParams(vmem_limit_bytes=60 * 2**20),
    )(*results)


def solution(mesh):
    return jax.shard_map(
        local,
        mesh=mesh,
        in_specs=(
            P(("dp", "node"), None),
            P(("dp", "node"), None),
            P(("dp", "node"), None),
            P(("dp", "node")),
            P("node", None),
            P("node"),
        ),
        out_specs=(P(("dp", "node"), None), P(("dp", "node"), None), P(("dp", "node"), None)),
        check_vma=False,
    )
```
